128 devices in a mesh: gx: 8 (over x_lo, z), gy: 16 (over y, x_hi, core).
Axes of the slice: x: 4 (x_hi: 2, x_lo: 2; x = x_hi * 2 + x_lo), y: 4, z: 4, core: 2. Of those that a mesh axis runs over, the one named last changes fastest.
Arguments:
- fine: bfloat16 [8192, 32, 512], P(('gx', 'gy')), may hold values from -6 to 6
- coarse: bfloat16 [1024, 32, 512], P(('gx', 'gy')), may hold values from -6 to 6
- weight: bfloat16 [27, 32, 32], replicated, may hold values from -0.21875 to 0.21875
- cotangent: bfloat16 [8192, 32, 512], P(('gx', 'gy')), may hold values from -6 to 6
- adjacency: int32 [8192, 27], P(('gx', 'gy')), may hold values from -1 to 575, as said below
- send_list: int32 [16384, 1], P(('gx', 'gy')), may hold values from -1 to 63, as said below
- child_src: int32 [8192], P(('gx', 'gy')), may hold values from -1 to 127, as said below
Outputs:
- block_out: bfloat16 [8192, 32, 512], P(('gx', 'gy'))
- fine_grad: bfloat16 [8192, 32, 512], P(('gx', 'gy'))
- coarse_grad: bfloat16 [1024, 32, 512], P(('gx', 'gy'))
- weight_grad: float32 [27, 32, 32], replicated
The draws below stay inside these ranges and needn't reach their ends.
Inputs may be any that keep to these rules, and one draw needn't show every extreme that they name: `adjacency`: entries follow the geometry of a grid of bricks: device (ix, iy) owns the brick columns x in [4 ix, 4 (ix + 1)), y in [4 iy, 4 (iy + 1)) and z layers 0 to 3, one slot a cell; an entry names a live brick at that displacement and never lies outside the mesh; neighbourhood is symmetric; entry 13 of a live slot is the slot itself; all entries of an empty slot are -1. Device 0 has every slot live. `send_list`: every octant id appears at most once on a device; it names the parent of exactly the fine slot whose child_src points at it. In every draw some device sends 1 octants to some device. child_src is -1 exactly for empty fine slots; no two fine slots of one device share a value.
All inputs are finite; a program needn't handle non-finite values.
Results may differ from the reference program's by a relative error of at most 0.0057.
Values may be sent and summed in bfloat16 or wider, within the bound.
No kernel may reach another device: no remote copies, remote signals or barrier semaphores. Data moves between devices by JAX's collectives and lax.ppermute only.
A program may use at most 320 MiB of HBM per device.

```python
import jax
import jax.numpy as jnp
from jax import lax

C = 32
SX = 4
SY = 4
SZ = 4
CAP = 64
CCAP = 8
SLOT = 1
TOTAL = 8192
CTOTAL = 1024
N_GX = 8
N_GY = 16


def layout(key):
    devices = N_GX * N_GY
    key_perm, key_live, key_dens, key_off = jax.random.split(key, 4)
    slot_table = jax.vmap(lambda subkey: jax.random.permutation(subkey, CAP))(jax.random.split(key_perm, devices))
    density = jax.random.randint(key_dens, (devices, 1), 3, 11)
    roll_draw = jax.random.randint(key_live, (devices, CAP), 0, 10)
    first_dev = (jnp.arange(devices) == 0)[:, None]
    alive_mask = (roll_draw < density) | (slot_table < 3 * SLOT) | first_dev
    order_draw = jax.random.permutation(key_off, devices)
    position = jnp.argsort(order_draw).astype(jnp.int32) + 3
    values = jnp.arange(devices, dtype=jnp.int32)
    score = jnp.where(values == devices // 2, 0, position)
    score = jnp.where(values == 1, 1, score)
    score = jnp.where(values == devices - 1, 2, score)
    offsets = jnp.argsort(score)[:CAP // SLOT]
    return (slot_table.astype(jnp.int32), alive_mask, offsets.astype(jnp.int32))


def slot_alive(slot_table, alive_mask):
    cell_of_slot = jnp.argsort(slot_table, axis=1)
    return jnp.take_along_axis(alive_mask, cell_of_slot, axis=1)


def draw_adjacency(key, part):
    slot_table, alive_mask, offsets = layout(key)
    devices = N_GX * N_GY
    cells = jnp.arange(CAP, dtype=jnp.int32)
    cell_x = cells // (SY * SZ)
    cell_y = cells // SZ % SY
    cell_z = cells % SZ
    dev_ids = jnp.arange(devices, dtype=jnp.int32)
    dev_x = (dev_ids // N_GY)[:, None]
    dev_y = (dev_ids % N_GY)[:, None]
    entries = []
    for off_x in (-1, 0, 1):
        for off_y in (-1, 0, 1):
            for off_z in (-1, 0, 1):
                glob_x = dev_x * SX + cell_x[None, :] + off_x
                glob_y = dev_y * SY + cell_y[None, :] + off_y
                glob_z = jnp.broadcast_to(cell_z[None, :] + off_z, glob_x.shape)
                inside = (glob_x >= 0) & (glob_x < SX * N_GX) & (glob_y >= 0) & (glob_y < SY * N_GY) & (glob_z >= 0) & (glob_z < SZ)
                safe_x = jnp.clip(glob_x, 0, SX * N_GX - 1)
                safe_y = jnp.clip(glob_y, 0, SY * N_GY - 1)
                safe_z = jnp.clip(glob_z, 0, SZ - 1)
                owner_x = safe_x // SX
                owner_y = safe_y // SY
                owner = owner_x * N_GY + owner_y
                cell_near = (safe_x % SX * SY + safe_y % SY) * SZ + safe_z
                slot_near = slot_table[owner, cell_near]
                live_near = alive_mask[owner, cell_near]
                place_code = (owner_x - dev_x + 1) * 3 + (owner_y - dev_y + 1)
                entries.append(jnp.where(inside & live_near & alive_mask, place_code * CAP + slot_near, -1))
    lookup = jnp.stack(entries, axis=-1)
    cell_of_slot = jnp.argsort(slot_table, axis=1)
    lookup = jnp.take_along_axis(lookup, cell_of_slot[:, :, None], axis=1)
    return lookup.reshape(devices * CAP, 27).astype(jnp.int32)


def draw_child_src(key, part):
    slot_table, alive_mask, offsets = layout(key)
    devices = N_GX * N_GY
    live_slot = slot_alive(slot_table, alive_mask)
    fine_slot = jnp.arange(CAP, dtype=jnp.int32)
    source = (jnp.arange(devices, dtype=jnp.int32)[:, None] + offsets[fine_slot // SLOT][None, :]) % devices
    result = jnp.where(live_slot, source * SLOT + (fine_slot % SLOT)[None, :], -1)
    return result.reshape(devices * CAP).astype(jnp.int32)


def draw_send_list(key, part):
    slot_table, alive_mask, offsets = layout(key)
    devices = N_GX * N_GY
    live_slot = slot_alive(slot_table, alive_mask)
    fine_slot = jnp.arange(CAP, dtype=jnp.int32)
    dest = jnp.broadcast_to(jnp.arange(devices, dtype=jnp.int32)[:, None], (devices, CAP))
    source = (dest + offsets[fine_slot // SLOT][None, :]) % devices
    within = jnp.broadcast_to((fine_slot % SLOT)[None, :], (devices, CAP))
    values = jnp.where(live_slot, jnp.broadcast_to(fine_slot[None, :], (devices, CAP)), -1)
    lookup = jnp.full((devices, devices, SLOT), -1, jnp.int32).at[source, dest, within].set(values)
    return lookup.reshape(devices * devices, SLOT).astype(jnp.int32)


def steps_of(rng, dims, cuts, least, high):
    def one(dim, shards_of):
        steps = jax.random.uniform(jax.random.fold_in(jax.random.fold_in(rng, 6), dim), (shards_of,), jnp.float32, least / len(cuts), high / len(cuts))
        return jnp.repeat(jnp.exp(steps), dims[dim] // shards_of).reshape((-1,) + (1,) * (len(dims) - dim - 1))

    gain = one(*cuts[0])
    for cut in cuts[1:]:
        gain = gain * one(*cut)
    return gain


def centred(key, extent, width, limit, shards=(), kind=jnp.bfloat16):
    values = jax.random.normal(key, extent, jnp.float32) * width
    if len(shards) > 0:
        values = steps_of(key, extent, shards, -0.22, 0.18) * values
    return jnp.clip(values, min=-limit, max=limit).astype(kind)


def setup_inputs(seed: int = 0) -> dict:
    key_of = jax.random.split(jax.random.key(seed), 8)
    return {
        "fine": centred(key_of[0], (TOTAL, C, 512), 1.0, 6.0, ((0, 128),)),
        "coarse": centred(key_of[1], (CTOTAL, C, 512), 1.0, 6.0, ((0, 128),)),
        "weight": centred(key_of[2], (27, C, C), (27 * C) ** -0.5, 0.21875),
        "cotangent": centred(key_of[3], (TOTAL, C, 512), 1.0, 6.0, ((0, 128),)),
        "adjacency": draw_adjacency(jax.random.fold_in(key_of[7], 71), 0),
        "send_list": draw_send_list(jax.random.fold_in(key_of[7], 71), 0),
        "child_src": draw_child_src(jax.random.fold_in(key_of[7], 71), 0),
    }


offset_list = [(off_x, off_y, off_z) for off_x in (-1, 0, 1) for off_y in (-1, 0, 1) for off_z in (-1, 0, 1)]
shift_list = [off_x * 100 + off_y * 10 + off_z for (off_x, off_y, off_z) in offset_list]
window_start = 111
window_len = 778
row_block = 64


def span(offset):
    if offset < 0:
        return (7, 8)
    if offset == 0:
        return (0, 8)
    return (0, 1)


def interior(values):
    leading = values.shape[:-1]
    padded = jnp.pad(values, [(0, 0)] * len(leading) + [(0, 22)])
    padded = padded.reshape(leading + (8, 100))[..., :80]
    return padded.reshape(leading + (8, 8, 10))[..., :8].reshape(leading + (512,))


def spread(values):
    leading = values.shape[:-1]
    volume = values.reshape(leading + (8, 8, 8))
    volume = jnp.pad(volume, [(0, 0)] * len(leading) + [(0, 0), (0, 0), (0, 2)]).reshape(leading + (8, 80))
    volume = jnp.pad(volume, [(0, 0)] * len(leading) + [(0, 0), (0, 20)]).reshape(leading + (800,))
    return volume[..., :window_len]


def silu_slope(preact):
    sigma = jax.nn.sigmoid(preact)
    return sigma * (1.0 + preact * (1.0 - sigma))


def stitch(portions):
    planes = []
    for off_x in (-1, 0, 1):
        strips = []
        for off_y in (-1, 0, 1):
            strips.append(jnp.concatenate([portions[(off_x, off_y, off_z)] for off_z in (-1, 0, 1)], axis=4))
        planes.append(jnp.concatenate(strips, axis=3))
    return jnp.concatenate(planes, axis=2)


def assemble(bricks, neighbour):
    brick_total, channels = bricks.shape[0], bricks.shape[1]
    portions = {}
    for position, (off_x, off_y, off_z) in enumerate(offset_list):
        span_x, span_y, span_z = span(off_x), span(off_y), span(off_z)
        own_part = bricks[:, :, span_x[0]:span_x[1], span_y[0]:span_y[1], span_z[0]:span_z[1]]
        if position == 13:
            portions[(off_x, off_y, off_z)] = own_part
        else:
            lookup = jnp.concatenate([own_part, jnp.zeros_like(own_part[:1])], axis=0)
            portions[(off_x, off_y, off_z)] = jnp.take(lookup, neighbour[:, position], axis=0)
    return stitch(portions).reshape(brick_total, channels, 1000)


def columns(padded, direction):
    return jnp.stack([lax.slice_in_dim(padded, window_start + direction * offset_flat, window_start + direction * offset_flat + window_len, axis=2) for offset_flat in shift_list], axis=1)


def reference(fine, coarse, weight, cotangent, adjacency, send_list, child_src):
    brick_total, channels = fine.shape[0], fine.shape[1]
    devices = N_GX * N_GY
    coarse_total = coarse.shape[0]
    row_ids = jnp.arange(brick_total, dtype=jnp.int32)
    home_dev = row_ids // CAP
    alive_mask = (adjacency[:, 13] >= 0).astype(jnp.float32)
    place_code = jnp.where(adjacency < 0, 0, adjacency) // CAP
    slot_code = jnp.where(adjacency < 0, 0, adjacency) % CAP
    near_x = (home_dev // N_GY)[:, None] + place_code // 3 - 1
    near_y = (home_dev % N_GY)[:, None] + place_code % 3 - 1
    target = (near_x * N_GY + near_y) * CAP + slot_code
    neighbour = jnp.where(adjacency < 0, brick_total, target).astype(jnp.int32)

    octants = coarse.reshape(coarse_total, channels, 2, 4, 2, 4, 2, 4).transpose(0, 2, 4, 6, 1, 3, 5, 7).reshape(coarse_total * 8, channels, 64)
    safe_src = jnp.where(child_src < 0, 0, child_src)
    source = safe_src // SLOT
    within = safe_src % SLOT
    octant_id = send_list[source * devices + home_dev, within]
    octant_row = jnp.where(child_src < 0, coarse_total * 8, source * (CCAP * 8) + octant_id).astype(jnp.int32)
    octant_table = jnp.concatenate([octants, jnp.zeros_like(octants[:1])], axis=0)
    parents = jnp.take(octant_table, octant_row, axis=0).reshape(brick_total, channels, 4, 4, 4)
    upsampled = jnp.repeat(jnp.repeat(jnp.repeat(parents, 2, axis=2), 2, axis=3), 2, axis=4)
    alive5 = alive_mask[:, None, None, None, None]
    hidden = ((fine.astype(jnp.float32).reshape(brick_total, channels, 8, 8, 8) + upsampled.astype(jnp.float32)) * alive5).astype(jnp.bfloat16)

    padded_h = assemble(hidden, neighbour)
    blocks = brick_total // row_block
    weight32 = weight.astype(jnp.float32)

    def forward_rows(inputs):
        padded_block, hidden_block, cot_block, alive_block = inputs
        stacked = columns(padded_block, 1).astype(jnp.float32)
        preact = interior(jnp.einsum("koc,bkcp->bop", weight32, stacked))
        mixed_out = ((hidden_block.astype(jnp.float32) + jax.nn.silu(preact)) * alive_block).astype(jnp.bfloat16)
        grad_pre = (cot_block.astype(jnp.float32) * silu_slope(preact) * alive_block).astype(jnp.bfloat16)
        return mixed_out, grad_pre

    block_out, grad_pre = lax.map(forward_rows, (
        padded_h.reshape(blocks, row_block, channels, 1000),
        hidden.reshape(blocks, row_block, channels, 512),
        cotangent.reshape(blocks, row_block, channels, 512),
        alive_mask.reshape(blocks, row_block, 1, 1)))
    block_out = block_out.reshape(brick_total, channels, 512)
    grad_pre = grad_pre.reshape(brick_total, channels, 512)

    padded_d = assemble(grad_pre.reshape(brick_total, channels, 8, 8, 8), neighbour)

    def backward_rows(running, inputs):
        padded_hb, padded_db, grad_block = inputs
        stacked_h = columns(padded_hb, 1).astype(jnp.float32)
        stacked_d = columns(padded_db, -1).astype(jnp.float32)
        running = running + jnp.einsum("bop,bkcp->koc", spread(grad_block.astype(jnp.float32)), stacked_h)
        back_conv = interior(jnp.einsum("koc,bkop->bcp", weight32, stacked_d))
        return running, back_conv

    weight_grad, back_conv = lax.scan(backward_rows, jnp.zeros((27, channels, channels), jnp.float32), (
        padded_h.reshape(blocks, row_block, channels, 1000),
        padded_d.reshape(blocks, row_block, channels, 1000),
        grad_pre.reshape(blocks, row_block, channels, 512)))
    back_conv = back_conv.reshape(brick_total, channels, 512)
    grad_hidden = (cotangent.astype(jnp.float32) + back_conv) * alive_mask[:, None, None]
    fine_grad = grad_hidden.astype(jnp.bfloat16)
    pooled = grad_hidden.reshape(brick_total, channels, 4, 2, 4, 2, 4, 2).sum(axis=(3, 5, 7)).astype(jnp.bfloat16).reshape(brick_total, channels, 64)
    octant_grad = jnp.zeros((coarse_total * 8 + 1, channels, 64), jnp.bfloat16).at[octant_row].set(pooled)[:-1]
    coarse_grad = octant_grad.reshape(coarse_total, 2, 2, 2, channels, 4, 4, 4).transpose(0, 4, 1, 5, 2, 6, 3, 7).reshape(coarse_total, channels, 512)
    return block_out, fine_grad, coarse_grad, weight_grad
```

```python
import jax
import jax.numpy as jnp
import numpy as np
from jax import lax
from jax.experimental import pallas as pl
from jax.experimental.pallas import tpu as pltpu
from jax.sharding import PartitionSpec as P

axes = ("gx", "gy")
channels = 32
capacity = 64
quad = 4
steps = capacity // quad
band = 9 * channels
depth = 10 * band
face_n = 16
corner_n = 4
side_n = face_n + 2 * corner_n
base_xm = capacity
base_xp = base_xm + face_n
base_ym = base_xp + face_n
base_yp = base_ym + side_n
zero_row = base_yp + side_n
table_rows = zero_row + 1
place_base = (
    base_ym + face_n,
    base_xm,
    base_yp + face_n,
    base_ym,
    0,
    base_yp,
    base_ym + face_n + corner_n,
    base_xp,
    base_yp + face_n + corner_n,
)
vmem = pl.BlockSpec(memory_space=pltpu.VMEM)
smem = pl.BlockSpec(memory_space=pltpu.SMEM)
bf16 = jnp.bfloat16
f32 = jnp.float32


def params():
    return pltpu.CompilerParams(vmem_limit_bytes=60 * 1024 * 1024)


def octant_matrix():
    out = np.zeros((512, 512), np.float32)
    for o in range(8):
        a, b, c = o // 4, o // 2 % 2, o % 2
        for v in range(64):
            x, y, z = v // 16, v // 4 % 4, v % 4
            out[(4 * a + x) * 64 + (4 * b + y) * 8 + 4 * c + z, o * 64 + v] = 1
    return out


def upsample_matrix():
    out = np.zeros((64, 512), np.float32)
    for p in range(512):
        x, y, z = p // 64, p // 8 % 8, p % 8
        out[(x // 2) * 16 + (y // 2) * 4 + z // 2, p] = 1
    wide = np.zeros((128, 1024), np.float32)
    wide[:64, :512] = out
    wide[64:, 512:] = out
    return wide


def y_face_matrix(y):
    out = np.zeros((512, 64), np.float32)
    for x in range(8):
        for z in range(8):
            out[x * 64 + y * 8 + z, x * 8 + z] = 1
    wide = np.zeros((1024, 128), np.float32)
    wide[:512, :64] = out
    wide[512:, 64:] = out
    return wide


def pool_matrix():
    out = np.zeros((4, 2, 128, 256), np.float32)
    for t in range(4):
        for b in range(4):
            for y in range(0, 8, 2):
                for z in range(0, 8, 2):
                    out[t, b // 2, (b % 2) * 64 + y * 8 + z, b * 64 + t * 16 + (y // 2) * 4 + z // 2] = 1
    return out.reshape(1024, 256)


def const(values):
    return jnp.asarray(values, dtype=bf16)


def lane_id(rows):
    return lax.broadcasted_iota(jnp.int32, (rows, 128), 1)


def roll(v, shift):
    return pltpu.roll(v, shift % 128, 1)


def octant_kernel(send, coarse, perm, out, tab):
    low = lane_id(16) < 64
    y = jnp.dot(coarse[...].reshape(256, 512), perm[...], preferred_element_type=f32).astype(bf16)
    for i in range(8):
        for g in range(4):
            part = y[i * 32 : i * 32 + 32, g * 128 : g * 128 + 128]
            tab[i * 8 + 2 * g] = jnp.where(low, part[:16], roll(part[16:], 64))
            tab[i * 8 + 2 * g + 1] = jnp.where(low, roll(part[:16], 64), part[16:])

    def body(i, carry):
        for j in range(8):
            d = i * 8 + j
            out[d] = tab[jnp.maximum(send[d], 0)]
        return carry

    lax.fori_loop(0, 16, body, 0)


def emit_faces(lists, bricks, ylow, yhigh, out_xm, out_xp, out_ym, out_yp, wide):
    low = lane_id(16) < 64
    for r in range(side_n):
        s = lists[r]
        out_xm[r] = jnp.where(low, bricks[s, 0:16, 0:128], roll(bricks[s, 16:32, 0:128], 64))
        s = lists[side_n + r]
        out_xp[r] = jnp.where(low, roll(bricks[s, 0:16, 384:512], 64), bricks[s, 16:32, 384:512])
    for side, (matrix, out) in enumerate(((ylow, out_ym), (yhigh, out_yp))):
        for r in range(face_n):
            s = lists[2 * side_n + side * face_n + r]
            wide[r * 16 : r * 16 + 16, 0:512] = bricks[s, 0:16, :]
            wide[r * 16 : r * 16 + 16, 512:1024] = bricks[s, 16:32, :]
        out[...] = (
            jnp.dot(wide[...], matrix[...], preferred_element_type=f32)
            .astype(bf16)
            .reshape(face_n, 16, 128)
        )


def hidden_kernel(
    child, alive, lists, incoming, fine, up, ylow, yhigh, hidden, xm, xp, ym, yp, wide
):
    def body(i, carry):
        rows = []
        for j in range(8):
            rows.append(incoming[jnp.maximum(child[i * 8 + j], 0)])
        big = jnp.dot(jnp.concatenate(rows, axis=0), up[...], preferred_element_type=f32)
        for j in range(8):
            s = i * 8 + j
            live = alive[s] > 0
            for h in range(2):
                total = fine[s, h * 16 : h * 16 + 16, :].astype(f32) + big[
                    j * 16 : j * 16 + 16, h * 512 : h * 512 + 512
                ]
                hidden[s, h * 16 : h * 16 + 16, :] = jnp.where(live, total, 0.0).astype(bf16)
        return carry

    lax.fori_loop(0, 8, body, 0)
    emit_faces(lists, hidden, ylow, yhigh, xm, xp, ym, yp, wide)


def fill_table(table, own, rxm, rxp, rym, ryp, elow, ehigh):
    def copy(i, carry):
        for j in range(8):
            table[i * 8 + j] = own[i * 8 + j]
        return carry

    lax.fori_loop(0, capacity // 8, copy, 0)
    for row, source, at in (
        [(base_xm + r, rxm, r) for r in range(face_n)]
        + [(base_ym + face_n + r, rym, face_n + r) for r in range(corner_n)]
        + [(base_yp + face_n + r, ryp, face_n + r) for r in range(corner_n)]
    ):
        table[row, 0:16, 384:512] = roll(source[at], 64)
        table[row, 16:32, 384:512] = source[at]
    for row, source, at in (
        [(base_xp + r, rxp, r) for r in range(face_n)]
        + [(base_ym + face_n + corner_n + r, rym, face_n + corner_n + r) for r in range(corner_n)]
        + [(base_yp + face_n + corner_n + r, ryp, face_n + corner_n + r) for r in range(corner_n)]
    ):
        table[row, 0:16, 0:128] = source[at]
        table[row, 16:32, 0:128] = roll(source[at], 64)
    for base, source, matrix in ((base_ym, rym, ehigh), (base_yp, ryp, elow)):
        big = jnp.dot(
            source[0:face_n].reshape(face_n * 16, 128), matrix[...], preferred_element_type=f32
        ).astype(bf16)
        for r in range(face_n):
            table[base + r, 0:16, :] = big[r * 16 : r * 16 + 16, 0:512]
            table[base + r, 16:32, :] = big[r * 16 : r * 16 + 16, 512:1024]
    table[zero_row] = jnp.zeros((channels, 512), bf16)


def to_pair(even_odd, low):
    first, second = even_odd
    return (
        jnp.where(low, first, roll(second, 64)),
        jnp.where(low, roll(first, 64), second),
    )


def build_stack(step, near, table, stack):
    lane = lane_id(channels)
    inner = lane & 63
    low = lane < 64
    y_first, y_last = inner < 8, inner >= 56
    z_first, z_last = (lane & 7) == 0, (lane & 7) == 7

    def sources(brick, off_x, tile):
        def at(off_y, off_z):
            row = near[brick * 27 + (off_x + 1) * 9 + (off_y + 1) * 3 + off_z + 1]
            return table[row, :, tile * 128 : tile * 128 + 128]

        return (
            at(0, 0),
            jnp.where(y_last, at(-1, 0), at(1, 0)),
            jnp.where(z_last, at(0, -1), at(0, 1)),
            jnp.where(
                y_last,
                jnp.where(z_last, at(-1, -1), at(-1, 1)),
                jnp.where(z_last, at(1, -1), at(1, 1)),
            ),
        )

    def shifts(plane, pair, kinds):
        own, near_y, near_z, near_yz = kinds
        own_z = (
            jnp.where(z_first, roll(near_z, -7), roll(own, 1)),
            own,
            jnp.where(z_last, roll(near_z, 7), roll(own, -1)),
        )
        next_z = (
            jnp.where(z_first, roll(near_yz, -7), roll(near_y, 1)),
            near_y,
            jnp.where(z_last, roll(near_yz, 7), roll(near_y, -1)),
        )
        for k in range(3):
            trio = (
                jnp.where(y_first, roll(next_z[k], -56), roll(own_z[k], 8)),
                own_z[k],
                jnp.where(y_last, roll(next_z[k], 56), roll(own_z[k], -8)),
            )
            for j in range(3):
                row = plane * band + (j * 3 + k) * channels
                stack[row : row + channels, pair * 128 : pair * 128 + 128] = trio[j]

    for pair in range(2):
        b0 = step * quad + 2 * pair
        for off_x, tile in ((-1, 3), (0, 0), (0, 1), (0, 2), (0, 3), (1, 0)):
            first = sources(b0, off_x, tile)
            second = sources(b0 + 1, off_x, tile)
            both = [to_pair(ab, low) for ab in zip(first, second)]
            if off_x <= 0:
                plane = 0 if off_x < 0 else 2 + 2 * tile
                shifts(plane, pair, [b[1] for b in both])
            if off_x >= 0:
                plane = 9 if off_x > 0 else 1 + 2 * tile
                shifts(plane, pair, [b[0] for b in both])


def alive_lanes(step, near):
    lane = lax.broadcasted_iota(jnp.int32, (1, 256), 1)
    out = jnp.zeros((1, 256), f32)
    for i in range(quad):
        live = (near[(step * quad + i) * 27 + 13] != zero_row).astype(f32)
        out = jnp.where(lane // 64 == i, live, out)
    return out


def quad_cotangent(cot, t, low):
    even, odd = [], []
    for pair in range(2):
        e, o = to_pair(
            (
                cot[2 * pair, :, t * 128 : t * 128 + 128],
                cot[2 * pair + 1, :, t * 128 : t * 128 + 128],
            ),
            low,
        )
        even.append(e)
        odd.append(o)
    return (
        jnp.concatenate(even, axis=1).astype(f32),
        jnp.concatenate(odd, axis=1).astype(f32),
    )


def from_pair(ref, at, even, odd, t, low):
    for pair in range(2):
        e = even[:, pair * 128 : pair * 128 + 128]
        o = odd[:, pair * 128 : pair * 128 + 128]
        ref[at + 2 * pair, :, t * 128 : t * 128 + 128] = jnp.where(low, e, roll(o, 64))
        ref[at + 2 * pair + 1, :, t * 128 : t * 128 + 128] = jnp.where(low, roll(e, 64), o)


def forward_kernel(
    near, lists, hidden, rxm, rxp, rym, ryp, cot, weight, elow, ehigh, ylow, yhigh,
    block_out, grad, stack_out, grad_pair, xm, xp, ym, yp, table, wide,
):
    step = pl.program_id(0)

    @pl.when(step == 0)
    def _():
        fill_table(table, hidden, rxm, rxp, rym, ryp, elow, ehigh)

    stack = stack_out.at[0]
    build_stack(step, near, table, stack)
    pre_all = jnp.dot(weight[...], stack[...], preferred_element_type=f32)
    low = lane_id(channels) < 64
    live = alive_lanes(step, near)
    for t in range(4):
        cots = quad_cotangent(cot, t, low)
        mixed, grads = [], []
        for p in range(2):
            x = 2 * t + p
            pre = pre_all[x * 32 : x * 32 + 32]
            row = (x + 1) * band + 4 * channels
            here = stack[row : row + channels, :].astype(f32)
            sigma = 0.5 * jnp.tanh(0.5 * pre) + 0.5
            mixed.append(((here + pre * sigma) * live).astype(bf16))
            grads.append((cots[p] * (sigma * (1.0 + pre * (1.0 - sigma))) * live).astype(bf16))
            grad_pair[0, x * 32 : x * 32 + 32, :] = grads[p]
        from_pair(block_out, 0, mixed[0], mixed[1], t, low)
        from_pair(grad, step * quad, grads[0], grads[1], t, low)

    @pl.when(step == steps - 1)
    def _():
        emit_faces(lists, grad, ylow, yhigh, xm, xp, ym, yp, wide)


def weight_kernel(stack, grad_pair, out, total, turned):
    step = pl.program_id(0)
    part = lax.dot_general(
        stack[0], grad_pair[0], (((1,), (1,)), ((), ())), preferred_element_type=f32
    )

    @pl.when(step == 0)
    def _():
        total[...] = part

    @pl.when(step > 0)
    def _():
        total[...] += part

    @pl.when(step == steps - 1)
    def _():
        acc = total[0 : 3 * band, 0:32]
        for x in range(1, 8):
            acc = acc + total[x * band : x * band + 3 * band, x * 32 : x * 32 + 32]
        turned[...] = jnp.zeros((1024, 128), f32)
        turned[0 : 3 * band, 0:32] = acc
        across = turned[...].T
        for j in range(4):
            out[j] = across[0:32, j * 256 : j * 256 + 256]


def backward_kernel(
    near, child, grad, rxm, rxp, rym, ryp, cot, weight, elow, ehigh, pool,
    fine_grad, back, table,
):
    step = pl.program_id(0)

    @pl.when(step == 0)
    def _():
        fill_table(table[0], grad, rxm, rxp, rym, ryp, elow, ehigh)
        back[...] = jnp.zeros_like(back)

    stack = table[1]
    build_stack(step, near, table[0], stack)
    conv = jnp.dot(weight[...], stack[...], preferred_element_type=f32)
    low = lane_id(channels) < 64
    low16 = lane_id(16) < 64
    live = alive_lanes(step, near)
    sums = []
    for t in range(4):
        cots = quad_cotangent(cot, t, low)
        full = [
            (cots[p] + conv[(2 * t + p) * 32 : (2 * t + p) * 32 + 32]) * live for p in range(2)
        ]
        from_pair(fine_grad, 0, full[0].astype(bf16), full[1].astype(bf16), t, low)
        both = full[0] + full[1]
        for pair in range(2):
            v = both[:, pair * 128 : pair * 128 + 128]
            v = v + roll(v, -1)
            v = v + roll(v, -8)
            sums.append(v.astype(bf16))
    pooled = jnp.dot(
        jnp.concatenate(sums, axis=1), pool[...], preferred_element_type=f32
    ).astype(bf16)
    for i in range(quad):
        tile = pooled[:, (i // 2) * 128 : (i // 2) * 128 + 128]
        if i % 2 == 0:
            packed = jnp.where(low16, tile[:16], roll(tile[16:], 64))
        else:
            packed = jnp.where(low16, roll(tile[:16], 64), tile[16:])
        target = child[step * quad + i]

        @pl.when(target >= 0)
        def _():
            back[target] = packed


def last_kernel(send, returned, totals, perm, coarse_grad, weight_grad, tab):
    low = lane_id(16) < 64
    tab[...] = jnp.zeros_like(tab)

    def body(i, carry):
        for j in range(8):
            d = i * 8 + j
            target = send[d]

            @pl.when(target >= 0)
            def _():
                tab[target] = returned[d]

        return carry

    lax.fori_loop(0, 16, body, 0)
    rows = []
    for i in range(8):
        tops, bottoms = [], []
        for g in range(4):
            a, b = tab[i * 8 + 2 * g], tab[i * 8 + 2 * g + 1]
            tops.append(jnp.where(low, a, roll(b, 64)))
            bottoms.append(jnp.where(low, roll(a, 64), b))
        rows.append(jnp.concatenate(tops, axis=1))
        rows.append(jnp.concatenate(bottoms, axis=1))
    spread = jnp.dot(jnp.concatenate(rows, axis=0), perm[...], preferred_element_type=f32)
    coarse_grad[...] = spread.astype(bf16).reshape(8, 32, 512)
    for k in range(27):
        weight_grad[k] = totals[k // 8, :, (k % 8) * 32 : (k % 8) * 32 + 32]


def shape(dims, kind=bf16):
    return jax.ShapeDtypeStruct(dims, kind)


def ranks(flags):
    before = (jnp.arange(capacity)[:, None] < jnp.arange(capacity)[None, :]).astype(bf16)
    return jnp.dot(flags.astype(bf16), before, preferred_element_type=f32).astype(jnp.int32)


def indices(adjacency):
    table_id = jnp.arange(9 * capacity, dtype=jnp.int32)
    hits = adjacency[:, :, None] == table_id
    rank = ranks(hits.any(axis=(0, 1)).reshape(9, capacity)).reshape(-1)
    row_base = jnp.asarray(np.repeat(np.array(place_base), capacity), jnp.int32)
    own = (table_id // capacity) == 4
    row_of = jnp.where(own, table_id % capacity, row_base + rank)
    near = jnp.sum(jnp.where(hits, row_of, 0), axis=2)
    near = jnp.where(adjacency < 0, zero_row, near)
    place = jnp.where(adjacency < 0, -1, adjacency // capacity)
    need = (place[None, :, :] == jnp.arange(9)[:, None, None]).any(axis=2)
    order = ranks(need)
    slot = jnp.arange(capacity, dtype=jnp.int32)
    pick = need[:, None, :] & (order[:, None, :] == jnp.arange(face_n)[None, :, None])
    chosen = jnp.sum(jnp.where(pick, slot, 0), axis=2)
    lists = jnp.concatenate(
        [
            chosen[1], chosen[0, :corner_n], chosen[2, :corner_n],
            chosen[7], chosen[6, :corner_n], chosen[8, :corner_n],
            chosen[3], chosen[5],
        ]
    )
    return near.reshape(-1).astype(jnp.int32), lists.astype(jnp.int32)


def banded(taps):
    return jnp.concatenate(
        [jnp.pad(taps, ((0, 0), (x * band, (7 - x) * band))) for x in range(8)], axis=0
    )


def moved(value, shift_x, shift_y):
    count_x, count_y = lax.axis_size("gx"), lax.axis_size("gy")
    pairs = [
        (i * count_y + j, (i + shift_x) * count_y + j + shift_y)
        for i in range(count_x)
        for j in range(count_y)
        if 0 <= i + shift_x < count_x and 0 <= j + shift_y < count_y
    ]
    return lax.ppermute(value, axes, pairs)


def halo(xm, xp, ym, yp):
    from_xm = moved(xp, 1, 0)
    from_xp = moved(xm, -1, 0)
    mid = face_n + corner_n
    up = jnp.concatenate([yp, from_xm[mid:], from_xp[mid:]], axis=0)
    down = jnp.concatenate([ym, from_xm[face_n:mid], from_xp[face_n:mid]], axis=0)
    from_ym = moved(up, 0, 1)
    from_yp = moved(down, 0, -1)
    return from_xm, from_xp, from_ym, from_yp


def exchange(value):
    return lax.all_to_all(value, axes, split_axis=0, concat_axis=0, tiled=True)


def whole(dims):
    return pl.BlockSpec(dims, lambda i: (0,) * len(dims))


def on_device(fine, coarse, weight, cotangent, adjacency, send_list, child_src):
    devices = lax.axis_size("gx") * lax.axis_size("gy")
    send = send_list.reshape(-1)
    perm = const(octant_matrix())
    perm_t = const(octant_matrix().T)
    y_low, y_high = y_face_matrix(0), y_face_matrix(7)
    ylow, yhigh = const(y_low), const(y_high)
    elow, ehigh = const(y_low.T), const(y_high.T)
    up = const(upsample_matrix())
    pool = const(pool_matrix())
    packed = (16, 128)
    side = shape((side_n,) + packed)
    face = shape((face_n,) + packed)

    outgoing = pl.pallas_call(
        octant_kernel,
        out_shape=shape((devices,) + packed),
        in_specs=[smem, vmem, vmem],
        out_specs=vmem,
        scratch_shapes=[pltpu.VMEM((64,) + packed, bf16)],
        compiler_params=params(),
        name="octants",
    )(send, coarse, perm)
    incoming = exchange(outgoing)

    near, lists = indices(adjacency)
    alive = (adjacency[:, 13] >= 0).astype(jnp.int32)
    taps = banded(weight.transpose(1, 0, 2).reshape(channels, 27 * channels))
    back_taps = banded(weight[::-1].transpose(2, 0, 1).reshape(channels, 27 * channels))

    hidden, xm, xp, ym, yp = pl.pallas_call(
        hidden_kernel,
        out_shape=(shape((capacity, channels, 512)), side, side, face, face),
        in_specs=[smem, smem, smem] + [vmem] * 5,
        out_specs=(vmem,) * 5,
        scratch_shapes=[pltpu.VMEM((face_n * 16, 1024), bf16)],
        compiler_params=params(),
        name="hidden",
    )(child_src, alive, lists, incoming, fine, up, ylow, yhigh)
    near_h = halo(xm, xp, ym, yp)

    bricks = whole((capacity, channels, 512))
    sides = [whole((n,) + packed) for n in (side_n, side_n, side_n, side_n)]
    per_quad = pl.BlockSpec((quad, channels, 512), lambda i: (i, 0, 0))
    stack_spec = pl.BlockSpec((1, depth, 256), lambda i: (i, 0, 0))
    pair_spec = pl.BlockSpec((1, 256, 256), lambda i: (i, 0, 0))
    table = pltpu.VMEM((table_rows, channels, 512), bf16)
    block_out, grad, stacks, grad_pair, gxm, gxp, gym, gyp = pl.pallas_call(
        forward_kernel,
        grid=(steps,),
        out_shape=(
            shape((capacity, channels, 512)),
            shape((capacity, channels, 512)),
            shape((steps, depth, 256)),
            shape((steps, 256, 256)),
            side, side, face, face,
        ),
        in_specs=[smem, smem, bricks]
        + sides
        + [per_quad, whole((256, depth))]
        + [whole((128, 1024))] * 2
        + [whole((1024, 128))] * 2,
        out_specs=(per_quad, bricks, stack_spec, pair_spec)
        + tuple(whole((n,) + packed) for n in (side_n, side_n, face_n, face_n)),
        scratch_shapes=[table, pltpu.VMEM((face_n * 16, 1024), bf16)],
        compiler_params=params(),
        name="forward",
    )(near, lists, hidden, *near_h, cotangent, taps, elow, ehigh, ylow, yhigh)
    near_g = halo(gxm, gxp, gym, gyp)

    term = pl.pallas_call(
        weight_kernel,
        grid=(steps,),
        out_shape=shape((4, 32, 256), f32),
        in_specs=[stack_spec, pair_spec],
        out_specs=whole((4, 32, 256)),
        scratch_shapes=[pltpu.VMEM((depth, 256), f32), pltpu.VMEM((1024, 128), f32)],
        compiler_params=params(),
        name="weight_term",
    )(stacks, grad_pair)
    terms = exchange(term.reshape(128, 256))
    mine = jnp.sum(terms, axis=0)
    totals = exchange(jnp.broadcast_to(mine[None, :], (devices, 256))).reshape(4, 32, 256)

    fine_grad, back = pl.pallas_call(
        backward_kernel,
        grid=(steps,),
        out_shape=(shape((capacity, channels, 512)), shape((devices,) + packed)),
        in_specs=[smem, smem, bricks]
        + sides
        + [per_quad, whole((256, depth)), whole((128, 1024)), whole((128, 1024))]
        + [whole((1024, 256))],
        out_specs=(per_quad, whole((devices,) + packed)),
        scratch_shapes=[[table, pltpu.VMEM((depth, 256), bf16)]],
        compiler_params=params(),
        name="backward",
    )(near, child_src, grad, *near_g, cotangent, back_taps, elow, ehigh, pool)
    returned = exchange(back)

    coarse_grad, weight_grad = pl.pallas_call(
        last_kernel,
        out_shape=(shape((8, channels, 512)), shape((27, channels, channels), f32)),
        in_specs=[smem, vmem, vmem, vmem],
        out_specs=(vmem, vmem),
        scratch_shapes=[pltpu.VMEM((64,) + packed, bf16)],
        compiler_params=params(),
        name="coarse",
    )(send, returned, totals, perm_t)
    return block_out, fine_grad, coarse_grad, weight_grad


def solution(mesh):
    return jax.shard_map(
        on_device,
        mesh=mesh,
        in_specs=(
            P(axes, None, None),
            P(axes, None, None),
            P(),
            P(axes, None, None),
            P(axes, None),
            P(axes, None),
            P(axes),
        ),
        out_specs=(
            P(axes, None, None),
            P(axes, None, None),
            P(axes, None, None),
            P(),
        ),
        check_vma=False,
    )
```

```python
import jax
import jax.numpy as jnp
import numpy as np
from jax import lax
from jax.experimental import pallas as pl
from jax.experimental.pallas import tpu as pltpu
from jax.sharding import PartitionSpec as P

axes = ("gx", "gy")
channels = 32
capacity = 64
quad = 4
steps = capacity // quad
band = 9 * channels
depth = 10 * band
face_n = 16
corner_n = 4
side_n = face_n + 2 * corner_n
base_xm = capacity
base_xp = base_xm + face_n
base_ym = base_xp + face_n
base_yp = base_ym + side_n
zero_row = base_yp + side_n
table_rows = zero_row + 1
place_base = (
    base_ym + face_n,
    base_xm,
    base_yp + face_n,
    base_ym,
    0,
    base_yp,
    base_ym + face_n + corner_n,
    base_xp,
    base_yp + face_n + corner_n,
)
vmem = pl.BlockSpec(memory_space=pltpu.VMEM)
smem = pl.BlockSpec(memory_space=pltpu.SMEM)
bf16 = jnp.bfloat16
f32 = jnp.float32


def params():
    return pltpu.CompilerParams(vmem_limit_bytes=60 * 1024 * 1024)


def octant_matrix():
    out = np.zeros((512, 512), np.float32)
    for o in range(8):
        a, b, c = o // 4, o // 2 % 2, o % 2
        for v in range(64):
            x, y, z = v // 16, v // 4 % 4, v % 4
            out[(4 * a + x) * 64 + (4 * b + y) * 8 + 4 * c + z, o * 64 + v] = 1
    return out


def upsample_matrix():
    out = np.zeros((64, 512), np.float32)
    for p in range(512):
        x, y, z = p // 64, p // 8 % 8, p % 8
        out[(x // 2) * 16 + (y // 2) * 4 + z // 2, p] = 1
    wide = np.zeros((128, 1024), np.float32)
    wide[:64, :512] = out
    wide[64:, 512:] = out
    return wide


def y_face_matrix(y):
    out = np.zeros((512, 64), np.float32)
    for x in range(8):
        for z in range(8):
            out[x * 64 + y * 8 + z, x * 8 + z] = 1
    wide = np.zeros((1024, 128), np.float32)
    wide[:512, :64] = out
    wide[512:, 64:] = out
    return wide


def pool_matrix():
    out = np.zeros((4, 2, 128, 256), np.float32)
    for t in range(4):
        for b in range(4):
            for y in range(0, 8, 2):
                for z in range(0, 8, 2):
                    out[t, b // 2, (b % 2) * 64 + y * 8 + z, b * 64 + t * 16 + (y // 2) * 4 + z // 2] = 1
    return out.reshape(1024, 256)


def const(values):
    return jnp.asarray(values, dtype=bf16)


def lane_id(rows):
    return lax.broadcasted_iota(jnp.int32, (rows, 128), 1)


def roll(v, shift):
    return pltpu.roll(v, shift % 128, 1)


def octant_kernel(send, coarse, perm, out, tab):
    low = lane_id(16) < 64
    y = jnp.dot(coarse[...].reshape(256, 512), perm[...], preferred_element_type=f32).astype(bf16)
    for i in range(8):
        for g in range(4):
            part = y[i * 32 : i * 32 + 32, g * 128 : g * 128 + 128]
            tab[i * 8 + 2 * g] = jnp.where(low, part[:16], roll(part[16:], 64))
            tab[i * 8 + 2 * g + 1] = jnp.where(low, roll(part[:16], 64), part[16:])

    def body(i, carry):
        for j in range(8):
            d = i * 8 + j
            out[d] = tab[jnp.maximum(send[d], 0)]
        return carry

    lax.fori_loop(0, 16, body, 0)


def emit_faces(lists, bricks, ylow, yhigh, out_xm, out_xp, out_ym, out_yp, wide):
    low = lane_id(16) < 64
    for r in range(side_n):
        s = lists[r]
        out_xm[r] = jnp.where(low, bricks[s, 0:16, 0:128], roll(bricks[s, 16:32, 0:128], 64))
        s = lists[side_n + r]
        out_xp[r] = jnp.where(low, roll(bricks[s, 0:16, 384:512], 64), bricks[s, 16:32, 384:512])
    for side, (matrix, out) in enumerate(((ylow, out_ym), (yhigh, out_yp))):
        for r in range(face_n):
            s = lists[2 * side_n + side * face_n + r]
            wide[r * 16 : r * 16 + 16, 0:512] = bricks[s, 0:16, :]
            wide[r * 16 : r * 16 + 16, 512:1024] = bricks[s, 16:32, :]
        out[...] = (
            jnp.dot(wide[...], matrix[...], preferred_element_type=f32)
            .astype(bf16)
            .reshape(face_n, 16, 128)
        )


def hidden_kernel(
    child, alive, lists, incoming, fine, up, ylow, yhigh, hidden, xm, xp, ym, yp, wide
):
    def body(i, carry):
        rows = []
        for j in range(8):
            rows.append(incoming[jnp.maximum(child[i * 8 + j], 0)])
        big = jnp.dot(jnp.concatenate(rows, axis=0), up[...], preferred_element_type=f32)
        for j in range(8):
            s = i * 8 + j
            live = alive[s] > 0
            for h in range(2):
                total = fine[s, h * 16 : h * 16 + 16, :].astype(f32) + big[
                    j * 16 : j * 16 + 16, h * 512 : h * 512 + 512
                ]
                hidden[s, h * 16 : h * 16 + 16, :] = jnp.where(live, total, 0.0).astype(bf16)
        return carry

    lax.fori_loop(0, 8, body, 0)
    emit_faces(lists, hidden, ylow, yhigh, xm, xp, ym, yp, wide)


def fill_table(table, own, rxm, rxp, rym, ryp, elow, ehigh):
    def copy(i, carry):
        for j in range(8):
            table[i * 8 + j] = own[i * 8 + j]
        return carry

    lax.fori_loop(0, capacity // 8, copy, 0)
    for row, source, at in (
        [(base_xm + r, rxm, r) for r in range(face_n)]
        + [(base_ym + face_n + r, rym, face_n + r) for r in range(corner_n)]
        + [(base_yp + face_n + r, ryp, face_n + r) for r in range(corner_n)]
    ):
        table[row, 0:16, 384:512] = roll(source[at], 64)
        table[row, 16:32, 384:512] = source[at]
    for row, source, at in (
        [(base_xp + r, rxp, r) for r in range(face_n)]
        + [(base_ym + face_n + corner_n + r, rym, face_n + corner_n + r) for r in range(corner_n)]
        + [(base_yp + face_n + corner_n + r, ryp, face_n + corner_n + r) for r in range(corner_n)]
    ):
        table[row, 0:16, 0:128] = source[at]
        table[row, 16:32, 0:128] = roll(source[at], 64)
    for base, source, matrix in ((base_ym, rym, ehigh), (base_yp, ryp, elow)):
        big = jnp.dot(
            source[0:face_n].reshape(face_n * 16, 128), matrix[...], preferred_element_type=f32
        ).astype(bf16)
        for r in range(face_n):
            table[base + r, 0:16, :] = big[r * 16 : r * 16 + 16, 0:512]
            table[base + r, 16:32, :] = big[r * 16 : r * 16 + 16, 512:1024]
    table[zero_row] = jnp.zeros((channels, 512), bf16)


def to_pair(even_odd, low):
    first, second = even_odd
    return (
        jnp.where(low, first, roll(second, 64)),
        jnp.where(low, roll(first, 64), second),
    )


def shift_matrix():
    out = np.zeros((256, 256), np.float32)
    for lane in range(128):
        z = lane % 8
        out[lane - 1 if z > 0 else 128 + lane + 7, lane] = 1
        out[lane + 1 if z < 7 else 128 + lane - 7, 128 + lane] = 1
    return out


def build_stack(index, near, table, shift, kinds, turned, stack):
    lane = lane_id(channels)
    inner = lane & 63
    low = lane < 64
    y_first, y_last = inner < 8, inner >= 56
    z_last = (lane & 7) == 7

    def sources(brick, off_x, tile):
        def at(off_y, off_z):
            row = near[brick * 27 + (off_x + 1) * 9 + (off_y + 1) * 3 + off_z + 1]
            return table[row, :, tile * 128 : tile * 128 + 128]

        return (
            at(0, 0),
            jnp.where(z_last, at(0, -1), at(0, 1)),
            jnp.where(y_last, at(-1, 0), at(1, 0)),
            jnp.where(
                y_last,
                jnp.where(z_last, at(-1, -1), at(-1, 1)),
                jnp.where(z_last, at(1, -1), at(1, 1)),
            ),
        )

    for pair in range(2):
        b0 = index * quad + 2 * pair
        for off_x, tile in ((-1, 3), (0, 0), (0, 1), (0, 2), (0, 3), (1, 0)):
            first = sources(b0, off_x, tile)
            second = sources(b0 + 1, off_x, tile)
            for kind in range(4):
                swap = kind >= 2
                even, odd = to_pair(
                    (second[kind], first[kind]) if swap else (first[kind], second[kind]), low
                )
                base = (2 * pair + kind // 2) * 320
                at_lane = (kind % 2) * 128
                if off_x <= 0:
                    row = base + (0 if off_x < 0 else 2 + 2 * tile) * channels
                    kinds[row : row + channels, at_lane : at_lane + 128] = odd
                if off_x >= 0:
                    row = base + (9 if off_x > 0 else 1 + 2 * tile) * channels
                    kinds[row : row + channels, at_lane : at_lane + 128] = even
    turned[...] = jnp.dot(kinds[...], shift[...], preferred_element_type=f32).astype(bf16)
    for pair in range(2):
        for plane in range(10):
            own_row = 2 * pair * 320 + plane * channels
            far_row = own_row + 320
            for k in range(3):
                source, at_lane = ((turned, 0), (kinds, 0), (turned, 128))[k]
                own = source[own_row : own_row + channels, at_lane : at_lane + 128]
                far = source[far_row : far_row + channels, at_lane : at_lane + 128]
                trio = (
                    roll(jnp.where(y_last, far, own), 8),
                    own,
                    roll(jnp.where(y_first, far, own), -8),
                )
                for j in range(3):
                    row = plane * band + (j * 3 + k) * channels
                    stack[row : row + channels, pair * 128 : pair * 128 + 128] = trio[j]


def alive_lanes(step, near):
    lane = lax.broadcasted_iota(jnp.int32, (1, 256), 1)
    out = jnp.zeros((1, 256), f32)
    for i in range(quad):
        live = (near[(step * quad + i) * 27 + 13] != zero_row).astype(f32)
        out = jnp.where(lane // 64 == i, live, out)
    return out


def quad_cotangent(cot, at, t, low):
    even, odd = [], []
    for pair in range(2):
        e, o = to_pair(
            (
                cot[at + 2 * pair, :, t * 128 : t * 128 + 128],
                cot[at + 2 * pair + 1, :, t * 128 : t * 128 + 128],
            ),
            low,
        )
        even.append(e)
        odd.append(o)
    return (
        jnp.concatenate(even, axis=1).astype(f32),
        jnp.concatenate(odd, axis=1).astype(f32),
    )


def from_pair(ref, at, even, odd, t, low):
    for pair in range(2):
        e = even[:, pair * 128 : pair * 128 + 128]
        o = odd[:, pair * 128 : pair * 128 + 128]
        ref[at + 2 * pair, :, t * 128 : t * 128 + 128] = jnp.where(low, e, roll(o, 64))
        ref[at + 2 * pair + 1, :, t * 128 : t * 128 + 128] = jnp.where(low, roll(e, 64), o)


def forward_kernel(
    near, lists, hidden, rxm, rxp, rym, ryp, cot, weight, elow, ehigh, ylow, yhigh, shift,
    block_out, grad, term, xm, xp, ym, yp,
    table, wide, kinds, turned, stacks, total, term_wide,
):
    step = pl.program_id(0)

    def build(index, slot):
        build_stack(index, near, table, shift, kinds[slot], turned[slot], stacks[slot])

    @pl.when(step == 0)
    def _():
        fill_table(table, hidden, rxm, rxp, rym, ryp, elow, ehigh)
        total[...] = jnp.zeros_like(total)
        build(0, 0)

    low = lane_id(channels) < 64

    def process(index, slot):
        stack = stacks[slot]
        pre_all = jnp.dot(weight[...], stack[...], preferred_element_type=f32)
        live = alive_lanes(index, near)
        grad_pair = []
        for t in range(4):
            cots = quad_cotangent(cot, slot * quad, t, low)
            mixed, grads = [], []
            for p in range(2):
                x = 2 * t + p
                pre = pre_all[x * 32 : x * 32 + 32]
                row = (x + 1) * band + 4 * channels
                here = stack[row : row + channels, :].astype(f32)
                sigma = 0.5 * jnp.tanh(0.5 * pre) + 0.5
                mixed.append(((here + pre * sigma) * live).astype(bf16))
                grads.append((cots[p] * (sigma * (1.0 + pre * (1.0 - sigma))) * live).astype(bf16))
            from_pair(block_out, slot * quad, mixed[0], mixed[1], t, low)
            from_pair(grad, index * quad, grads[0], grads[1], t, low)
            grad_pair += grads
        grad_all = jnp.concatenate(grad_pair, axis=0)
        for x in range(10):
            total[x * band : x * band + band] += lax.dot_general(
                stack[x * band : x * band + band],
                grad_all,
                (((1,), (1,)), ((), ())),
                preferred_element_type=f32,
            )

    build(2 * step + 1, 1)
    process(2 * step, 0)
    build(jnp.minimum(2 * step + 2, steps - 1), 0)
    process(2 * step + 1, 1)

    @pl.when(step == steps // 2 - 1)
    def _():
        emit_faces(lists, grad, ylow, yhigh, xm, xp, ym, yp, wide)
        acc = total[0 : 3 * band, 0:32]
        for x in range(1, 8):
            acc = acc + total[x * band : x * band + 3 * band, x * 32 : x * 32 + 32]
        term_wide[...] = jnp.zeros((1024, 128), f32)
        term_wide[0 : 3 * band, 0:32] = acc
        across = term_wide[...].T
        for j in range(4):
            term[j] = across[0:32, j * 256 : j * 256 + 256]


def backward_kernel(
    near, child, grad, rxm, rxp, rym, ryp, cot, weight, elow, ehigh, pool, shift, terms,
    fine_grad, back,
    table, kinds, turned, stacks, octants,
):
    step = pl.program_id(0)

    def build(index, slot):
        build_stack(index, near, table, shift, kinds[slot], turned[slot], stacks[slot])

    @pl.when(step == 0)
    def _():
        fill_table(table, grad, rxm, rxp, rym, ryp, elow, ehigh)
        build(0, 0)
        rest = jnp.sum(terms[...], axis=0, keepdims=True)
        rows = []
        for i in range(3):
            part = rest.astype(bf16)
            rest = rest - part.astype(f32)
            rows += [part[:, 0:128].astype(f32), part[:, 128:256].astype(f32)]
        rows += [jnp.zeros((2, 128), f32)]
        tail = jnp.concatenate(rows, axis=0).astype(bf16)
        clear = jnp.zeros((16, 128), bf16)

        def body(i, carry):
            for j in range(8):
                back[i * 8 + j, 0:16, :] = clear
                back[i * 8 + j, 16:24, :] = tail
            return carry

        lax.fori_loop(0, 16, body, 0)

    low = lane_id(channels) < 64
    low16 = lane_id(16) < 64

    def process(index, slot):
        conv = jnp.dot(weight[...], stacks[slot][...], preferred_element_type=f32)
        live = alive_lanes(index, near)
        sums = []
        for t in range(4):
            cots = quad_cotangent(cot, slot * quad, t, low)
            full = [
                (cots[p] + conv[(2 * t + p) * 32 : (2 * t + p) * 32 + 32]) * live
                for p in range(2)
            ]
            from_pair(fine_grad, slot * quad, full[0].astype(bf16), full[1].astype(bf16), t, low)
            both = full[0] + full[1]
            for pair in range(2):
                v = both[:, pair * 128 : pair * 128 + 128]
                v = v + roll(v, -1)
                v = v + roll(v, -8)
                sums.append(v.astype(bf16))
        pooled = jnp.dot(
            jnp.concatenate(sums, axis=1), pool[...], preferred_element_type=f32
        ).astype(bf16)
        for i in range(quad):
            tile = pooled[:, (i // 2) * 128 : (i // 2) * 128 + 128]
            if i % 2 == 0:
                packed = jnp.where(low16, tile[:16], roll(tile[16:], 64))
            else:
                packed = jnp.where(low16, roll(tile[:16], 64), tile[16:])
            octants[index * quad + i] = packed

    build(2 * step + 1, 1)
    process(2 * step, 0)
    build(jnp.minimum(2 * step + 2, steps - 1), 0)
    process(2 * step + 1, 1)

    @pl.when(step == steps // 2 - 1)
    def _():
        def body(i, carry):
            for j in range(8):
                target = child[i * 8 + j]

                @pl.when(target >= 0)
                def _():
                    back[target, 0:16, :] = octants[i * 8 + j]

            return carry

        lax.fori_loop(0, capacity // 8, body, 0)


def last_kernel(send, returned, perm, coarse_grad, weight_grad, tab, parts):
    low = lane_id(16) < 64
    tab[...] = jnp.zeros_like(tab)

    def body(i, carry):
        for j in range(8):
            d = i * 8 + j
            target = send[d]

            @pl.when(target >= 0)
            def _():
                tab[target] = returned[d, 0:16, :]

        return carry

    lax.fori_loop(0, 16, body, 0)
    rows = []
    for i in range(8):
        tops, bottoms = [], []
        for g in range(4):
            a, b = tab[i * 8 + 2 * g], tab[i * 8 + 2 * g + 1]
            tops.append(jnp.where(low, a, roll(b, 64)))
            bottoms.append(jnp.where(low, roll(a, 64), b))
        rows.append(jnp.concatenate(tops, axis=1))
        rows.append(jnp.concatenate(bottoms, axis=1))
    spread = jnp.dot(jnp.concatenate(rows, axis=0), perm[...], preferred_element_type=f32)
    coarse_grad[...] = spread.astype(bf16).reshape(8, 32, 512)
    parts[...] = returned[:, 16:24, :].astype(f32)
    for half in range(2):
        total = parts[:, half, :] + parts[:, half + 2, :] + parts[:, half + 4, :]
        for j in range(4):
            for i in range(4):
                k = j * 8 + half * 4 + i
                if k < 27:
                    weight_grad[k] = total[j * 32 : j * 32 + 32, i * 32 : i * 32 + 32]


def shape(dims, kind=bf16):
    return jax.ShapeDtypeStruct(dims, kind)


def ranks(flags):
    before = (jnp.arange(capacity)[:, None] < jnp.arange(capacity)[None, :]).astype(bf16)
    return jnp.dot(flags.astype(bf16), before, preferred_element_type=f32).astype(jnp.int32)


def indices(adjacency):
    table_id = jnp.arange(9 * capacity, dtype=jnp.int32)
    hits = adjacency[:, :, None] == table_id
    rank = ranks(hits.any(axis=(0, 1)).reshape(9, capacity)).reshape(-1)
    row_base = jnp.asarray(np.repeat(np.array(place_base), capacity), jnp.int32)
    own = (table_id // capacity) == 4
    row_of = jnp.where(own, table_id % capacity, row_base + rank)
    near = jnp.sum(jnp.where(hits, row_of, 0), axis=2)
    near = jnp.where(adjacency < 0, zero_row, near)
    place = jnp.where(adjacency < 0, -1, adjacency // capacity)
    need = (place[None, :, :] == jnp.arange(9)[:, None, None]).any(axis=2)
    order = ranks(need)
    slot = jnp.arange(capacity, dtype=jnp.int32)
    pick = need[:, None, :] & (order[:, None, :] == jnp.arange(face_n)[None, :, None])
    chosen = jnp.sum(jnp.where(pick, slot, 0), axis=2)
    lists = jnp.concatenate(
        [
            chosen[1], chosen[0, :corner_n], chosen[2, :corner_n],
            chosen[7], chosen[6, :corner_n], chosen[8, :corner_n],
            chosen[3], chosen[5],
        ]
    )
    return near.reshape(-1).astype(jnp.int32), lists.astype(jnp.int32)


def banded(taps):
    return jnp.concatenate(
        [jnp.pad(taps, ((0, 0), (x * band, (7 - x) * band))) for x in range(8)], axis=0
    )


def moved(value, shift_x, shift_y):
    count_x, count_y = lax.axis_size("gx"), lax.axis_size("gy")
    pairs = [
        (i * count_y + j, (i + shift_x) * count_y + j + shift_y)
        for i in range(count_x)
        for j in range(count_y)
        if 0 <= i + shift_x < count_x and 0 <= j + shift_y < count_y
    ]
    return lax.ppermute(value, axes, pairs)


def halo(xm, xp, ym, yp):
    from_xm = moved(xp, 1, 0)
    from_xp = moved(xm, -1, 0)
    mid = face_n + corner_n
    up = jnp.concatenate([yp, from_xm[mid:], from_xp[mid:]], axis=0)
    down = jnp.concatenate([ym, from_xm[face_n:mid], from_xp[face_n:mid]], axis=0)
    from_ym = moved(up, 0, 1)
    from_yp = moved(down, 0, -1)
    return from_xm, from_xp, from_ym, from_yp


def exchange(value):
    return lax.all_to_all(value, axes, split_axis=0, concat_axis=0, tiled=True)


def whole(dims):
    return pl.BlockSpec(dims, lambda i: (0,) * len(dims))


def on_device(fine, coarse, weight, cotangent, adjacency, send_list, child_src):
    devices = lax.axis_size("gx") * lax.axis_size("gy")
    send = send_list.reshape(-1)
    perm = const(octant_matrix())
    perm_t = const(octant_matrix().T)
    y_low, y_high = y_face_matrix(0), y_face_matrix(7)
    ylow, yhigh = const(y_low), const(y_high)
    elow, ehigh = const(y_low.T), const(y_high.T)
    up = const(upsample_matrix())
    pool = const(pool_matrix())
    shift = const(shift_matrix())
    packed = (16, 128)
    side = shape((side_n,) + packed)
    face = shape((face_n,) + packed)

    outgoing = pl.pallas_call(
        octant_kernel,
        out_shape=shape((devices,) + packed),
        in_specs=[smem, vmem, vmem],
        out_specs=vmem,
        scratch_shapes=[pltpu.VMEM((64,) + packed, bf16)],
        compiler_params=params(),
        name="octants",
    )(send, coarse, perm)
    incoming = exchange(outgoing)

    near, lists = indices(adjacency)
    alive = (adjacency[:, 13] >= 0).astype(jnp.int32)
    taps = banded(weight.transpose(1, 0, 2).reshape(channels, 27 * channels))
    back_taps = banded(weight[::-1].transpose(2, 0, 1).reshape(channels, 27 * channels))

    hidden, xm, xp, ym, yp = pl.pallas_call(
        hidden_kernel,
        out_shape=(shape((capacity, channels, 512)), side, side, face, face),
        in_specs=[smem, smem, smem] + [vmem] * 5,
        out_specs=(vmem,) * 5,
        scratch_shapes=[pltpu.VMEM((face_n * 16, 1024), bf16)],
        compiler_params=params(),
        name="hidden",
    )(child_src, alive, lists, incoming, fine, up, ylow, yhigh)
    near_h = halo(xm, xp, ym, yp)

    bricks = whole((capacity, channels, 512))
    sides = [whole((side_n,) + packed)] * 4
    per_step = pl.BlockSpec((2 * quad, channels, 512), lambda i: (i, 0, 0))
    table = pltpu.VMEM((table_rows, channels, 512), bf16)
    wide = pltpu.VMEM((face_n * 16, 1024), bf16)
    work = [
        [pltpu.VMEM((1280, 256), bf16)] * 2,
        [pltpu.VMEM((1280, 256), bf16)] * 2,
        [pltpu.VMEM((depth, 256), bf16)] * 2,
    ]
    block_out, grad, term, gxm, gxp, gym, gyp = pl.pallas_call(
        forward_kernel,
        grid=(steps // 2,),
        out_shape=(
            shape((capacity, channels, 512)),
            shape((capacity, channels, 512)),
            shape((4, 32, 256), f32),
            side, side, face, face,
        ),
        in_specs=[smem, smem, bricks]
        + sides
        + [per_step, whole((256, depth))]
        + [whole((128, 1024))] * 2
        + [whole((1024, 128))] * 2
        + [whole((256, 256))],
        out_specs=(per_step, bricks, whole((4, 32, 256)))
        + tuple(whole((n,) + packed) for n in (side_n, side_n, face_n, face_n)),
        scratch_shapes=[table, wide]
        + work
        + [pltpu.VMEM((depth, 256), f32), pltpu.VMEM((1024, 128), f32)],
        compiler_params=params(),
        name="forward",
    )(near, lists, hidden, *near_h, cotangent, taps, elow, ehigh, ylow, yhigh, shift)
    near_g = halo(gxm, gxp, gym, gyp)
    terms = exchange(term.reshape(devices, 256))

    fine_grad, back = pl.pallas_call(
        backward_kernel,
        grid=(steps // 2,),
        out_shape=(shape((capacity, channels, 512)), shape((devices, 24, 128))),
        in_specs=[smem, smem, bricks]
        + sides
        + [per_step, whole((256, depth)), whole((128, 1024)), whole((128, 1024))]
        + [whole((1024, 256)), whole((256, 256)), whole((devices, 256))],
        out_specs=(per_step, whole((devices, 24, 128))),
        scratch_shapes=[table] + work + [pltpu.VMEM((capacity,) + packed, bf16)],
        compiler_params=params(),
        name="backward",
    )(near, child_src, grad, *near_g, cotangent, back_taps, elow, ehigh, pool, shift, terms)
    returned = exchange(back)

    coarse_grad, weight_grad = pl.pallas_call(
        last_kernel,
        out_shape=(shape((8, channels, 512)), shape((27, channels, channels), f32)),
        in_specs=[smem, vmem, vmem],
        out_specs=(vmem, vmem),
        scratch_shapes=[pltpu.VMEM((64,) + packed, bf16), pltpu.VMEM((devices, 8, 128), f32)],
        compiler_params=params(),
        name="coarse",
    )(send, returned, perm_t)
    return block_out, fine_grad, coarse_grad, weight_grad


def solution(mesh):
    return jax.shard_map(
        on_device,
        mesh=mesh,
        in_specs=(
            P(axes, None, None),
            P(axes, None, None),
            P(),
            P(axes, None, None),
            P(axes, None),
            P(axes, None),
            P(axes),
        ),
        out_specs=(
            P(axes, None, None),
            P(axes, None, None),
            P(axes, None, None),
            P(),
        ),
        check_vma=False,
    )
```

```python
import jax
import jax.numpy as jnp
import numpy as np
from jax import lax
from jax.experimental import pallas as pl
from jax.experimental.pallas import tpu as pltpu
from jax.sharding import PartitionSpec as P

axes = ("gx", "gy")
channels = 32
capacity = 64
quad = 4
steps = capacity // quad
band = 9 * channels
depth = 10 * band
face_n = 16
corner_n = 4
side_n = face_n + 2 * corner_n
base_xm = capacity
base_xp = base_xm + face_n
base_ym = base_xp + face_n
base_yp = base_ym + side_n
zero_row = base_yp + side_n
table_rows = zero_row + 1
place_base = (
    base_ym + face_n,
    base_xm,
    base_yp + face_n,
    base_ym,
    0,
    base_yp,
    base_ym + face_n + corner_n,
    base_xp,
    base_yp + face_n + corner_n,
)
vmem = pl.BlockSpec(memory_space=pltpu.VMEM)
smem = pl.BlockSpec(memory_space=pltpu.SMEM)
bf16 = jnp.bfloat16
f32 = jnp.float32


def params():
    return pltpu.CompilerParams(vmem_limit_bytes=60 * 1024 * 1024)


def octant_matrix():
    out = np.zeros((512, 512), np.float32)
    for o in range(8):
        a, b, c = o // 4, o // 2 % 2, o % 2
        for v in range(64):
            x, y, z = v // 16, v // 4 % 4, v % 4
            out[(4 * a + x) * 64 + (4 * b + y) * 8 + 4 * c + z, o * 64 + v] = 1
    return out


def upsample_matrix():
    out = np.zeros((64, 512), np.float32)
    for p in range(512):
        x, y, z = p // 64, p // 8 % 8, p % 8
        out[(x // 2) * 16 + (y // 2) * 4 + z // 2, p] = 1
    wide = np.zeros((128, 1024), np.float32)
    wide[:64, :512] = out
    wide[64:, 512:] = out
    return wide


def y_face_matrix(y):
    out = np.zeros((512, 64), np.float32)
    for x in range(8):
        for z in range(8):
            out[x * 64 + y * 8 + z, x * 8 + z] = 1
    wide = np.zeros((1024, 128), np.float32)
    wide[:512, :64] = out
    wide[512:, 64:] = out
    return wide


def pool_matrix():
    out = np.zeros((4, 2, 128, 256), np.float32)
    for t in range(4):
        for b in range(4):
            for y in range(0, 8, 2):
                for z in range(0, 8, 2):
                    out[t, b // 2, (b % 2) * 64 + y * 8 + z, b * 64 + t * 16 + (y // 2) * 4 + z // 2] = 1
    return out.reshape(1024, 256)


def const(values):
    return jnp.asarray(values, dtype=bf16)


def lane_id(rows):
    return lax.broadcasted_iota(jnp.int32, (rows, 128), 1)


def roll(v, shift):
    return pltpu.roll(v, shift % 128, 1)


def octant_kernel(send, coarse, perm, out, tab):
    low = lane_id(16) < 64
    y = jnp.dot(coarse[...].reshape(256, 512), perm[...], preferred_element_type=f32).astype(bf16)
    for i in range(8):
        for g in range(4):
            part = y[i * 32 : i * 32 + 32, g * 128 : g * 128 + 128]
            tab[i * 8 + 2 * g] = jnp.where(low, part[:16], roll(part[16:], 64))
            tab[i * 8 + 2 * g + 1] = jnp.where(low, roll(part[:16], 64), part[16:])

    def body(i, carry):
        for j in range(8):
            d = i * 8 + j
            out[d] = tab[jnp.maximum(send[d], 0)]
        return carry

    lax.fori_loop(0, 16, body, 0)


def emit_faces(lists, bricks, ylow, yhigh, out_xm, out_xp, out_ym, out_yp, wide):
    low = lane_id(16) < 64
    for r in range(side_n):
        s = lists[r]
        out_xm[r] = jnp.where(low, bricks[s, 0:16, 0:128], roll(bricks[s, 16:32, 0:128], 64))
        s = lists[side_n + r]
        out_xp[r] = jnp.where(low, roll(bricks[s, 0:16, 384:512], 64), bricks[s, 16:32, 384:512])
    for side, (matrix, out) in enumerate(((ylow, out_ym), (yhigh, out_yp))):
        for r in range(face_n):
            s = lists[2 * side_n + side * face_n + r]
            wide[r * 16 : r * 16 + 16, 0:512] = bricks[s, 0:16, :]
            wide[r * 16 : r * 16 + 16, 512:1024] = bricks[s, 16:32, :]
        out[...] = (
            jnp.dot(wide[...], matrix[...], preferred_element_type=f32)
            .astype(bf16)
            .reshape(face_n, 16, 128)
        )


def hidden_kernel(
    child, alive, lists, incoming, fine, up, ylow, yhigh, hidden, xm, xp, ym, yp, wide, full
):
    step = pl.program_id(0)
    rows = []
    for j in range(16):
        rows.append(incoming[jnp.maximum(child[step * 16 + j], 0)])
    big = jnp.dot(jnp.concatenate(rows, axis=0), up[...], preferred_element_type=f32)
    for j in range(16):
        s = step * 16 + j
        live = (alive[s] > 0).astype(f32)
        for h in range(2):
            total = fine[j, h * 16 : h * 16 + 16, :].astype(f32) + big[
                j * 16 : j * 16 + 16, h * 512 : h * 512 + 512
            ]
            value = (total * live).astype(bf16)
            hidden[j, h * 16 : h * 16 + 16, :] = value
            full[s, h * 16 : h * 16 + 16, :] = value

    @pl.when(step == pl.num_programs(0) - 1)
    def _():
        emit_faces(lists, full, ylow, yhigh, xm, xp, ym, yp, wide)


def fill_table(table, own, rxm, rxp, rym, ryp, elow, ehigh):
    def copy(i, carry):
        for j in range(8):
            table[i * 8 + j] = own[i * 8 + j]
        return carry

    lax.fori_loop(0, capacity // 8, copy, 0)
    for row, source, at in (
        [(base_xm + r, rxm, r) for r in range(face_n)]
        + [(base_ym + face_n + r, rym, face_n + r) for r in range(corner_n)]
        + [(base_yp + face_n + r, ryp, face_n + r) for r in range(corner_n)]
    ):
        table[row, 0:16, 384:512] = roll(source[at], 64)
        table[row, 16:32, 384:512] = source[at]
    for row, source, at in (
        [(base_xp + r, rxp, r) for r in range(face_n)]
        + [(base_ym + face_n + corner_n + r, rym, face_n + corner_n + r) for r in range(corner_n)]
        + [(base_yp + face_n + corner_n + r, ryp, face_n + corner_n + r) for r in range(corner_n)]
    ):
        table[row, 0:16, 0:128] = source[at]
        table[row, 16:32, 0:128] = roll(source[at], 64)
    for base, source, matrix in ((base_ym, rym, ehigh), (base_yp, ryp, elow)):
        big = jnp.dot(
            source[0:face_n].reshape(face_n * 16, 128), matrix[...], preferred_element_type=f32
        ).astype(bf16)
        for r in range(face_n):
            table[base + r, 0:16, :] = big[r * 16 : r * 16 + 16, 0:512]
            table[base + r, 16:32, :] = big[r * 16 : r * 16 + 16, 512:1024]
    table[zero_row] = jnp.zeros((channels, 512), bf16)


def to_pair(even_odd, low):
    first, second = even_odd
    return (
        jnp.where(low, first, roll(second, 64)),
        jnp.where(low, roll(first, 64), second),
    )


def shift_matrix():
    out = np.zeros((256, 256), np.float32)
    for lane in range(128):
        z = lane % 8
        out[lane - 1 if z > 0 else 128 + lane + 7, lane] = 1
        out[lane + 1 if z < 7 else 128 + lane - 7, 128 + lane] = 1
    return out


def build_stack(index, near, table, shift, kinds, turned, stack):
    lane = lane_id(channels)
    inner = lane & 63
    low = lane < 64
    y_first, y_last = inner < 8, inner >= 56
    z_last = (lane & 7) == 7

    def sources(brick, off_x, tile):
        def at(off_y, off_z):
            row = near[brick * 27 + (off_x + 1) * 9 + (off_y + 1) * 3 + off_z + 1]
            return table[row, :, tile * 128 : tile * 128 + 128]

        return (
            at(0, 0),
            jnp.where(z_last, at(0, -1), at(0, 1)),
            jnp.where(y_last, at(-1, 0), at(1, 0)),
            jnp.where(
                y_last,
                jnp.where(z_last, at(-1, -1), at(-1, 1)),
                jnp.where(z_last, at(1, -1), at(1, 1)),
            ),
        )

    for pair in range(2):
        b0 = index * quad + 2 * pair
        for off_x, tile in ((-1, 3), (0, 0), (0, 1), (0, 2), (0, 3), (1, 0)):
            first = sources(b0, off_x, tile)
            second = sources(b0 + 1, off_x, tile)
            for kind in range(4):
                swap = kind >= 2
                even, odd = to_pair(
                    (second[kind], first[kind]) if swap else (first[kind], second[kind]), low
                )
                base = (2 * pair + kind // 2) * 320
                at_lane = (kind % 2) * 128
                if off_x <= 0:
                    row = base + (0 if off_x < 0 else 2 + 2 * tile) * channels
                    kinds[row : row + channels, at_lane : at_lane + 128] = odd
                if off_x >= 0:
                    row = base + (9 if off_x > 0 else 1 + 2 * tile) * channels
                    kinds[row : row + channels, at_lane : at_lane + 128] = even
    turned[...] = jnp.dot(kinds[...], shift[...], preferred_element_type=f32).astype(bf16)
    for pair in range(2):
        for plane in range(10):
            own_row = 2 * pair * 320 + plane * channels
            far_row = own_row + 320
            for k in range(3):
                source, at_lane = ((turned, 0), (kinds, 0), (turned, 128))[k]
                own = source[own_row : own_row + channels, at_lane : at_lane + 128]
                far = source[far_row : far_row + channels, at_lane : at_lane + 128]
                trio = (
                    roll(jnp.where(y_last, far, own), 8),
                    own,
                    roll(jnp.where(y_first, far, own), -8),
                )
                for j in range(3):
                    row = plane * band + (j * 3 + k) * channels
                    stack[row : row + channels, pair * 128 : pair * 128 + 128] = trio[j]


def banded(taps, weight):
    weight[...] = jnp.zeros_like(weight)
    for x in range(8):
        weight[x * 32 : x * 32 + 32, x * band : x * band + 3 * band] = taps[...]


def alive_lanes(step, near):
    lane = lax.broadcasted_iota(jnp.int32, (1, 256), 1)
    out = jnp.zeros((1, 256), f32)
    for i in range(quad):
        live = (near[(step * quad + i) * 27 + 13] != zero_row).astype(f32)
        out = jnp.where(lane // 64 == i, live, out)
    return out


def quad_cotangent(cot, at, t, low):
    even, odd = [], []
    for pair in range(2):
        e, o = to_pair(
            (
                cot[at + 2 * pair, :, t * 128 : t * 128 + 128],
                cot[at + 2 * pair + 1, :, t * 128 : t * 128 + 128],
            ),
            low,
        )
        even.append(e)
        odd.append(o)
    return (
        jnp.concatenate(even, axis=1).astype(f32),
        jnp.concatenate(odd, axis=1).astype(f32),
    )


def from_pair(ref, at, even, odd, t, low):
    for pair in range(2):
        e = even[:, pair * 128 : pair * 128 + 128]
        o = odd[:, pair * 128 : pair * 128 + 128]
        ref[at + 2 * pair, :, t * 128 : t * 128 + 128] = jnp.where(low, e, roll(o, 64))
        ref[at + 2 * pair + 1, :, t * 128 : t * 128 + 128] = jnp.where(low, roll(e, 64), o)


def forward_kernel(
    near, lists, hidden, rxm, rxp, rym, ryp, cot, taps, elow, ehigh, ylow, yhigh, shift,
    block_out, grad, term, xm, xp, ym, yp,
    table, weight, wide, kinds, turned, stacks, total, term_wide,
):
    step = pl.program_id(0)

    def build(index, slot):
        build_stack(index, near, table, shift, kinds[slot], turned[slot], stacks[slot])

    @pl.when(step == 0)
    def _():
        banded(taps, weight)
        fill_table(table, hidden, rxm, rxp, rym, ryp, elow, ehigh)
        total[...] = jnp.zeros_like(total)
        build(0, 0)

    low = lane_id(channels) < 64

    def process(index, slot):
        stack = stacks[slot]
        pre_all = jnp.dot(weight[...], stack[...], preferred_element_type=f32)
        live = alive_lanes(index, near)
        grad_pair = []
        for t in range(4):
            cots = quad_cotangent(cot, slot * quad, t, low)
            mixed, grads = [], []
            for p in range(2):
                x = 2 * t + p
                pre = pre_all[x * 32 : x * 32 + 32]
                row = (x + 1) * band + 4 * channels
                here = stack[row : row + channels, :].astype(f32)
                sigma = 0.5 * jnp.tanh(0.5 * pre) + 0.5
                mixed.append(((here + pre * sigma) * live).astype(bf16))
                grads.append((cots[p] * (sigma * (1.0 + pre * (1.0 - sigma))) * live).astype(bf16))
            from_pair(block_out, slot * quad, mixed[0], mixed[1], t, low)
            from_pair(grad, index * quad, grads[0], grads[1], t, low)
            grad_pair += grads
        grad_all = jnp.concatenate(grad_pair, axis=0)
        for x in range(10):
            total[x * band : x * band + band] += lax.dot_general(
                stack[x * band : x * band + band],
                grad_all,
                (((1,), (1,)), ((), ())),
                preferred_element_type=f32,
            )

    build(2 * step + 1, 1)
    process(2 * step, 0)
    build(jnp.minimum(2 * step + 2, steps - 1), 0)
    process(2 * step + 1, 1)

    @pl.when(step == steps // 2 - 1)
    def _():
        emit_faces(lists, grad, ylow, yhigh, xm, xp, ym, yp, wide)
        acc = total[0 : 3 * band, 0:32]
        for x in range(1, 8):
            acc = acc + total[x * band : x * band + 3 * band, x * 32 : x * 32 + 32]
        term_wide[...] = jnp.zeros((1024, 128), f32)
        term_wide[0 : 3 * band, 0:32] = acc
        across = term_wide[...].T
        for j in range(4):
            term[j] = across[0:32, j * 256 : j * 256 + 256]


def backward_kernel(
    near, child, grad, rxm, rxp, rym, ryp, cot, taps, elow, ehigh, pool, shift, terms,
    fine_grad, back,
    table, weight, kinds, turned, stacks, octants,
):
    step = pl.program_id(0)

    def build(index, slot):
        build_stack(index, near, table, shift, kinds[slot], turned[slot], stacks[slot])

    @pl.when(step == 0)
    def _():
        banded(taps, weight)
        fill_table(table, grad, rxm, rxp, rym, ryp, elow, ehigh)
        build(0, 0)
        rest = jnp.sum(terms[...], axis=0, keepdims=True)
        rows = []
        for i in range(3):
            part = rest.astype(bf16)
            rest = rest - part.astype(f32)
            rows += [part[:, 0:128].astype(f32), part[:, 128:256].astype(f32)]
        rows += [jnp.zeros((2, 128), f32)]
        tail = jnp.concatenate(rows, axis=0).astype(bf16)
        clear = jnp.zeros((16, 128), bf16)

        def body(i, carry):
            for j in range(8):
                back[i * 8 + j, 0:16, :] = clear
                back[i * 8 + j, 16:24, :] = tail
            return carry

        lax.fori_loop(0, 16, body, 0)

    low = lane_id(channels) < 64
    low16 = lane_id(16) < 64

    def process(index, slot):
        conv = jnp.dot(weight[...], stacks[slot][...], preferred_element_type=f32)
        live = alive_lanes(index, near)
        sums = []
        for t in range(4):
            cots = quad_cotangent(cot, slot * quad, t, low)
            full = [
                (cots[p] + conv[(2 * t + p) * 32 : (2 * t + p) * 32 + 32]) * live
                for p in range(2)
            ]
            from_pair(fine_grad, slot * quad, full[0].astype(bf16), full[1].astype(bf16), t, low)
            both = full[0] + full[1]
            for pair in range(2):
                v = both[:, pair * 128 : pair * 128 + 128]
                v = v + roll(v, -1)
                v = v + roll(v, -8)
                sums.append(v.astype(bf16))
        rows = pl.ds(pl.multiple_of(index * channels, channels), channels)
        for i in range(8):
            octants[rows, i * 128 : i * 128 + 128] = sums[i]

    build(2 * step + 1, 1)
    process(2 * step, 0)
    build(jnp.minimum(2 * step + 2, steps - 1), 0)
    process(2 * step + 1, 1)

    @pl.when(step == steps // 2 - 1)
    def _():
        pooled = jnp.dot(octants[...], pool[...], preferred_element_type=f32).astype(bf16)
        for s in range(capacity):
            row = s // quad * channels
            at_lane = (s % quad) // 2 * 128
            tile = pooled[row : row + channels, at_lane : at_lane + 128]
            if s % 2 == 0:
                packed = jnp.where(low16, tile[:16], roll(tile[16:], 64))
            else:
                packed = jnp.where(low16, roll(tile[:16], 64), tile[16:])
            back[child[s], 0:16, :] = packed


def last_kernel(send, returned, perm, coarse_grad, weight_grad, tab, parts):
    low = lane_id(16) < 64
    tab[...] = jnp.zeros_like(tab)

    def body(i, carry):
        for j in range(8):
            d = i * 8 + j
            target = send[d]

            @pl.when(target >= 0)
            def _():
                tab[target] = returned[d, 0:16, :]

        return carry

    lax.fori_loop(0, 16, body, 0)
    rows = []
    for i in range(8):
        tops, bottoms = [], []
        for g in range(4):
            a, b = tab[i * 8 + 2 * g], tab[i * 8 + 2 * g + 1]
            tops.append(jnp.where(low, a, roll(b, 64)))
            bottoms.append(jnp.where(low, roll(a, 64), b))
        rows.append(jnp.concatenate(tops, axis=1))
        rows.append(jnp.concatenate(bottoms, axis=1))
    spread = jnp.dot(jnp.concatenate(rows, axis=0), perm[...], preferred_element_type=f32)
    coarse_grad[...] = spread.astype(bf16).reshape(8, 32, 512)
    parts[...] = returned[:, 16:24, :].astype(f32)
    for half in range(2):
        total = parts[:, half, :] + parts[:, half + 2, :] + parts[:, half + 4, :]
        for j in range(4):
            for i in range(4):
                k = j * 8 + half * 4 + i
                if k < 27:
                    weight_grad[k] = total[j * 32 : j * 32 + 32, i * 32 : i * 32 + 32]


def shape(dims, kind=bf16):
    return jax.ShapeDtypeStruct(dims, kind)


def ranks(flags):
    before = (jnp.arange(capacity)[:, None] < jnp.arange(capacity)[None, :]).astype(bf16)
    return jnp.dot(flags.astype(bf16), before, preferred_element_type=f32).astype(jnp.int32)


def indices(adjacency):
    table_id = jnp.arange(9 * capacity, dtype=jnp.int32)
    hits = adjacency[:, :, None] == table_id
    rank = ranks(hits.any(axis=(0, 1)).reshape(9, capacity)).reshape(-1)
    row_base = jnp.asarray(np.repeat(np.array(place_base), capacity), jnp.int32)
    own = (table_id // capacity) == 4
    row_of = jnp.where(own, table_id % capacity, row_base + rank)
    near = jnp.sum(jnp.where(hits, row_of, 0), axis=2)
    near = jnp.where(adjacency < 0, zero_row, near)
    place = jnp.where(adjacency < 0, -1, adjacency // capacity)
    need = (place[None, :, :] == jnp.arange(9)[:, None, None]).any(axis=2)
    order = ranks(need)
    slot = jnp.arange(capacity, dtype=jnp.int32)
    pick = need[:, None, :] & (order[:, None, :] == jnp.arange(face_n)[None, :, None])
    chosen = jnp.sum(jnp.where(pick, slot, 0), axis=2)
    lists = jnp.concatenate(
        [
            chosen[1], chosen[0, :corner_n], chosen[2, :corner_n],
            chosen[7], chosen[6, :corner_n], chosen[8, :corner_n],
            chosen[3], chosen[5],
        ]
    )
    return near.reshape(-1).astype(jnp.int32), lists.astype(jnp.int32)


def moved(value, shift_x, shift_y):
    count_x, count_y = lax.axis_size("gx"), lax.axis_size("gy")
    pairs = [
        (i * count_y + j, (i + shift_x) * count_y + j + shift_y)
        for i in range(count_x)
        for j in range(count_y)
        if 0 <= i + shift_x < count_x and 0 <= j + shift_y < count_y
    ]
    return lax.ppermute(value, axes, pairs)


def halo(xm, xp, ym, yp):
    from_xm = moved(xp, 1, 0)
    from_xp = moved(xm, -1, 0)
    mid = face_n + corner_n
    up = jnp.concatenate([yp, from_xm[mid:], from_xp[mid:]], axis=0)
    down = jnp.concatenate([ym, from_xm[face_n:mid], from_xp[face_n:mid]], axis=0)
    from_ym = moved(up, 0, 1)
    from_yp = moved(down, 0, -1)
    return from_xm, from_xp, from_ym, from_yp


def exchange(value):
    return lax.all_to_all(value, axes, split_axis=0, concat_axis=0, tiled=True)


def whole(dims):
    return pl.BlockSpec(dims, lambda i: (0,) * len(dims))


def on_device(fine, coarse, weight, cotangent, adjacency, send_list, child_src):
    devices = lax.axis_size("gx") * lax.axis_size("gy")
    send = send_list.reshape(-1)
    perm = const(octant_matrix())
    perm_t = const(octant_matrix().T)
    y_low, y_high = y_face_matrix(0), y_face_matrix(7)
    ylow, yhigh = const(y_low), const(y_high)
    elow, ehigh = const(y_low.T), const(y_high.T)
    up = const(upsample_matrix())
    pool = const(pool_matrix())
    shift = const(shift_matrix())
    packed = (16, 128)
    side = shape((side_n,) + packed)
    face = shape((face_n,) + packed)

    outgoing = pl.pallas_call(
        octant_kernel,
        out_shape=shape((devices,) + packed),
        in_specs=[smem, vmem, vmem],
        out_specs=vmem,
        scratch_shapes=[pltpu.VMEM((64,) + packed, bf16)],
        compiler_params=params(),
        name="octants",
    )(send, coarse, perm)
    incoming = exchange(outgoing)

    near, lists = indices(adjacency)
    alive = (adjacency[:, 13] >= 0).astype(jnp.int32)
    sender = jnp.arange(devices, dtype=jnp.int32)
    unused = jnp.where((child_src[:, None] == sender).any(axis=0), devices, sender).min()
    back_to = jnp.where(child_src < 0, unused, child_src)
    taps = weight.transpose(1, 0, 2).reshape(channels, 27 * channels)
    back_taps = weight[::-1].transpose(2, 0, 1).reshape(channels, 27 * channels)

    part = pl.BlockSpec((16, channels, 512), lambda i: (i, 0, 0))
    hidden, xm, xp, ym, yp = pl.pallas_call(
        hidden_kernel,
        grid=(capacity // 16,),
        out_shape=(shape((capacity, channels, 512)), side, side, face, face),
        in_specs=[smem, smem, smem, whole((devices,) + packed), part]
        + [whole((128, 1024))]
        + [whole((1024, 128))] * 2,
        out_specs=(part,) + tuple(whole((n,) + packed) for n in (side_n, side_n, face_n, face_n)),
        scratch_shapes=[
            pltpu.VMEM((face_n * 16, 1024), bf16),
            pltpu.VMEM((capacity, channels, 512), bf16),
        ],
        compiler_params=params(),
        name="hidden",
    )(child_src, alive, lists, incoming, fine, up, ylow, yhigh)
    near_h = halo(xm, xp, ym, yp)

    bricks = whole((capacity, channels, 512))
    sides = [whole((side_n,) + packed)] * 4
    per_step = pl.BlockSpec((2 * quad, channels, 512), lambda i: (i, 0, 0))
    table = pltpu.VMEM((table_rows, channels, 512), bf16)
    wide = pltpu.VMEM((face_n * 16, 1024), bf16)
    banded_weight = pltpu.VMEM((256, depth), bf16)
    work = [
        [pltpu.VMEM((1280, 256), bf16)] * 2,
        [pltpu.VMEM((1280, 256), bf16)] * 2,
        [pltpu.VMEM((depth, 256), bf16)] * 2,
    ]
    block_out, grad, term, gxm, gxp, gym, gyp = pl.pallas_call(
        forward_kernel,
        grid=(steps // 2,),
        out_shape=(
            shape((capacity, channels, 512)),
            shape((capacity, channels, 512)),
            shape((4, 32, 256), f32),
            side, side, face, face,
        ),
        in_specs=[smem, smem, bricks]
        + sides
        + [per_step, whole((channels, 27 * channels))]
        + [whole((128, 1024))] * 2
        + [whole((1024, 128))] * 2
        + [whole((256, 256))],
        out_specs=(per_step, bricks, whole((4, 32, 256)))
        + tuple(whole((n,) + packed) for n in (side_n, side_n, face_n, face_n)),
        scratch_shapes=[table, banded_weight, wide]
        + work
        + [pltpu.VMEM((depth, 256), f32), pltpu.VMEM((1024, 128), f32)],
        compiler_params=params(),
        name="forward",
    )(near, lists, hidden, *near_h, cotangent, taps, elow, ehigh, ylow, yhigh, shift)
    near_g = halo(gxm, gxp, gym, gyp)
    terms = exchange(term.reshape(devices, 256))

    fine_grad, back = pl.pallas_call(
        backward_kernel,
        grid=(steps // 2,),
        out_shape=(shape((capacity, channels, 512)), shape((devices, 24, 128))),
        in_specs=[smem, smem, bricks]
        + sides
        + [per_step, whole((channels, 27 * channels)), whole((128, 1024)), whole((128, 1024))]
        + [whole((1024, 256)), whole((256, 256)), whole((devices, 256))],
        out_specs=(per_step, whole((devices, 24, 128))),
        scratch_shapes=[table, banded_weight] + work + [pltpu.VMEM((steps * channels, 1024), bf16)],
        compiler_params=params(),
        name="backward",
    )(near, back_to, grad, *near_g, cotangent, back_taps, elow, ehigh, pool, shift, terms)
    returned = exchange(back)

    coarse_grad, weight_grad = pl.pallas_call(
        last_kernel,
        out_shape=(shape((8, channels, 512)), shape((27, channels, channels), f32)),
        in_specs=[smem, vmem, vmem],
        out_specs=(vmem, vmem),
        scratch_shapes=[pltpu.VMEM((64,) + packed, bf16), pltpu.VMEM((devices, 8, 128), f32)],
        compiler_params=params(),
        name="coarse",
    )(send, returned, perm_t)
    return block_out, fine_grad, coarse_grad, weight_grad


def solution(mesh):
    return jax.shard_map(
        on_device,
        mesh=mesh,
        in_specs=(
            P(axes, None, None),
            P(axes, None, None),
            P(),
            P(axes, None, None),
            P(axes, None),
            P(axes, None),
            P(axes),
        ),
        out_specs=(
            P(axes, None, None),
            P(axes, None, None),
            P(axes, None, None),
            P(),
        ),
        check_vma=False,
    )
```

```python
import jax
import jax.numpy as jnp
import numpy as np
from jax import lax
from jax.experimental import pallas as pl
from jax.experimental.pallas import tpu as pltpu
from jax.sharding import PartitionSpec as P

axes = ("gx", "gy")
channels = 32
capacity = 64
quad = 4
steps = capacity // quad
band = 9 * channels
depth = 10 * band
face_n = 16
corner_n = 4
side_n = face_n + 2 * corner_n
base_xm = capacity
base_xp = base_xm + face_n
base_ym = base_xp + face_n
base_yp = base_ym + side_n
zero_row = base_yp + side_n
table_rows = zero_row + 1
place_base = (
    base_ym + face_n,
    base_xm,
    base_yp + face_n,
    base_ym,
    0,
    base_yp,
    base_ym + face_n + corner_n,
    base_xp,
    base_yp + face_n + corner_n,
)
vmem = pl.BlockSpec(memory_space=pltpu.VMEM)
smem = pl.BlockSpec(memory_space=pltpu.SMEM)
bf16 = jnp.bfloat16
f32 = jnp.float32


def params():
    return pltpu.CompilerParams(vmem_limit_bytes=60 * 1024 * 1024)


def octant_matrix():
    out = np.zeros((512, 512), np.float32)
    for o in range(8):
        a, b, c = o // 4, o // 2 % 2, o % 2
        for v in range(64):
            x, y, z = v // 16, v // 4 % 4, v % 4
            out[(4 * a + x) * 64 + (4 * b + y) * 8 + 4 * c + z, o * 64 + v] = 1
    return out


def upsample_matrix():
    out = np.zeros((64, 512), np.float32)
    for p in range(512):
        x, y, z = p // 64, p // 8 % 8, p % 8
        out[(x // 2) * 16 + (y // 2) * 4 + z // 2, p] = 1
    wide = np.zeros((128, 1024), np.float32)
    wide[:64, :512] = out
    wide[64:, 512:] = out
    return wide


def y_face_matrix(y):
    out = np.zeros((512, 64), np.float32)
    for x in range(8):
        for z in range(8):
            out[x * 64 + y * 8 + z, x * 8 + z] = 1
    wide = np.zeros((1024, 128), np.float32)
    wide[:512, :64] = out
    wide[512:, 64:] = out
    return wide


def pool_matrix():
    out = np.zeros((4, 2, 128, 256), np.float32)
    for t in range(4):
        for b in range(4):
            for y in range(0, 8, 2):
                for z in range(0, 8, 2):
                    out[t, b // 2, (b % 2) * 64 + y * 8 + z, b * 64 + t * 16 + (y // 2) * 4 + z // 2] = 1
    return out.reshape(1024, 256)


def const(values):
    return jnp.asarray(values, dtype=bf16)


def lane_id(rows):
    return lax.broadcasted_iota(jnp.int32, (rows, 128), 1)


def roll(v, shift):
    return pltpu.roll(v, shift % 128, 1)


def octant_kernel(send, coarse, perm, out, tab):
    low = lane_id(16) < 64
    y = jnp.dot(coarse[...].reshape(256, 512), perm[...], preferred_element_type=f32).astype(bf16)
    for i in range(8):
        for g in range(4):
            part = y[i * 32 : i * 32 + 32, g * 128 : g * 128 + 128]
            tab[i * 8 + 2 * g] = jnp.where(low, part[:16], roll(part[16:], 64))
            tab[i * 8 + 2 * g + 1] = jnp.where(low, roll(part[:16], 64), part[16:])

    def body(i, carry):
        for j in range(8):
            d = i * 8 + j
            out[d] = tab[jnp.maximum(send[d], 0)]
        return carry

    lax.fori_loop(0, 16, body, 0)


def emit_faces(lists, bricks, ylow, yhigh, out_xm, out_xp, out_ym, out_yp, wide):
    low = lane_id(16) < 64
    for r in range(side_n):
        s = lists[r]
        out_xm[r] = jnp.where(low, bricks[s, 0:16, 0:128], roll(bricks[s, 16:32, 0:128], 64))
        s = lists[side_n + r]
        out_xp[r] = jnp.where(low, roll(bricks[s, 0:16, 384:512], 64), bricks[s, 16:32, 384:512])
    for side, (matrix, out) in enumerate(((ylow, out_ym), (yhigh, out_yp))):
        for r in range(face_n):
            s = lists[2 * side_n + side * face_n + r]
            wide[r * 16 : r * 16 + 16, 0:512] = bricks[s, 0:16, :]
            wide[r * 16 : r * 16 + 16, 512:1024] = bricks[s, 16:32, :]
        out[...] = (
            jnp.dot(wide[...], matrix[...], preferred_element_type=f32)
            .astype(bf16)
            .reshape(face_n, 16, 128)
        )


def hidden_kernel(
    child, alive, lists, incoming, fine, up, ylow, yhigh, hidden, xm, xp, ym, yp, wide, full
):
    step = pl.program_id(0)
    rows = []
    for j in range(16):
        rows.append(incoming[jnp.maximum(child[step * 16 + j], 0)])
    big = jnp.dot(jnp.concatenate(rows, axis=0), up[...], preferred_element_type=f32)
    for j in range(16):
        s = step * 16 + j
        live = (alive[s] > 0).astype(f32)
        for h in range(2):
            total = fine[j, h * 16 : h * 16 + 16, :].astype(f32) + big[
                j * 16 : j * 16 + 16, h * 512 : h * 512 + 512
            ]
            value = (total * live).astype(bf16)
            hidden[j, h * 16 : h * 16 + 16, :] = value
            full[s, h * 16 : h * 16 + 16, :] = value

    @pl.when(step == pl.num_programs(0) - 1)
    def _():
        emit_faces(lists, full, ylow, yhigh, xm, xp, ym, yp, wide)


def fill_table(table, own, rxm, rxp, rym, ryp, elow, ehigh):
    def copy(i, carry):
        for j in range(8):
            table[i * 8 + j] = own[i * 8 + j]
        return carry

    lax.fori_loop(0, capacity // 8, copy, 0)
    for row, source, at in (
        [(base_xm + r, rxm, r) for r in range(face_n)]
        + [(base_ym + face_n + r, rym, face_n + r) for r in range(corner_n)]
        + [(base_yp + face_n + r, ryp, face_n + r) for r in range(corner_n)]
    ):
        table[row, 0:16, 384:512] = roll(source[at], 64)
        table[row, 16:32, 384:512] = source[at]
    for row, source, at in (
        [(base_xp + r, rxp, r) for r in range(face_n)]
        + [(base_ym + face_n + corner_n + r, rym, face_n + corner_n + r) for r in range(corner_n)]
        + [(base_yp + face_n + corner_n + r, ryp, face_n + corner_n + r) for r in range(corner_n)]
    ):
        table[row, 0:16, 0:128] = source[at]
        table[row, 16:32, 0:128] = roll(source[at], 64)
    for base, source, matrix in ((base_ym, rym, ehigh), (base_yp, ryp, elow)):
        big = jnp.dot(
            source[0:face_n].reshape(face_n * 16, 128), matrix[...], preferred_element_type=f32
        ).astype(bf16)
        for r in range(face_n):
            table[base + r, 0:16, :] = big[r * 16 : r * 16 + 16, 0:512]
            table[base + r, 16:32, :] = big[r * 16 : r * 16 + 16, 512:1024]
    table[zero_row] = jnp.zeros((channels, 512), bf16)


def to_pair(even_odd, low):
    first, second = even_odd
    return (
        jnp.where(low, first, roll(second, 64)),
        jnp.where(low, roll(first, 64), second),
    )


def shift_matrix():
    out = np.zeros((256, 256), np.float32)
    for lane in range(128):
        z = lane % 8
        out[lane - 1 if z > 0 else 128 + lane + 7, lane] = 1
        out[lane + 1 if z < 7 else 128 + lane - 7, 128 + lane] = 1
    return out


def build_stack(index, near, table, shift, kinds, turned, stack):
    lane = lane_id(channels)
    inner = lane & 63
    low = lane < 64
    y_first, y_last = inner < 8, inner >= 56
    z_last = (lane & 7) == 7

    def sources(brick, off_x, tile):
        def at(off_y, off_z):
            row = near[brick * 27 + (off_x + 1) * 9 + (off_y + 1) * 3 + off_z + 1]
            return table[row, :, tile * 128 : tile * 128 + 128]

        return (
            at(0, 0),
            jnp.where(z_last, at(0, -1), at(0, 1)),
            jnp.where(y_last, at(-1, 0), at(1, 0)),
            jnp.where(
                y_last,
                jnp.where(z_last, at(-1, -1), at(-1, 1)),
                jnp.where(z_last, at(1, -1), at(1, 1)),
            ),
        )

    for pair in range(2):
        b0 = index * quad + 2 * pair
        for off_x, tile in ((-1, 3), (0, 0), (0, 1), (0, 2), (0, 3), (1, 0)):
            first = sources(b0, off_x, tile)
            second = sources(b0 + 1, off_x, tile)
            for kind in range(4):
                swap = kind >= 2
                even, odd = to_pair(
                    (second[kind], first[kind]) if swap else (first[kind], second[kind]), low
                )
                base = (2 * pair + kind // 2) * 320
                at_lane = (kind % 2) * 128
                if off_x <= 0:
                    row = base + (0 if off_x < 0 else 2 + 2 * tile) * channels
                    kinds[row : row + channels, at_lane : at_lane + 128] = odd
                if off_x >= 0:
                    row = base + (9 if off_x > 0 else 1 + 2 * tile) * channels
                    kinds[row : row + channels, at_lane : at_lane + 128] = even
    turned[...] = jnp.dot(kinds[...], shift[...], preferred_element_type=f32).astype(bf16)
    for pair in range(2):
        for plane in range(10):
            own_row = 2 * pair * 320 + plane * channels
            far_row = own_row + 320
            for k in range(3):
                source, at_lane = ((turned, 0), (kinds, 0), (turned, 128))[k]
                own = source[own_row : own_row + channels, at_lane : at_lane + 128]
                far = source[far_row : far_row + channels, at_lane : at_lane + 128]
                trio = (
                    roll(jnp.where(y_last, far, own), 8),
                    own,
                    roll(jnp.where(y_first, far, own), -8),
                )
                for j in range(3):
                    row = plane * band + (j * 3 + k) * channels
                    stack[row : row + channels, pair * 128 : pair * 128 + 128] = trio[j]


def banded(taps, weight):
    weight[...] = jnp.zeros_like(weight)
    for x in range(8):
        weight[x * 32 : x * 32 + 32, x * band : x * band + 3 * band] = taps[...]


def convolve(weight, stack):
    halves = []
    for h in range(2):
        seen = slice(h * 4 * band, h * 4 * band + 6 * band)
        halves.append(
            jnp.dot(weight[h * 128 : h * 128 + 128, seen], stack[seen], preferred_element_type=f32)
        )
    return jnp.concatenate(halves, axis=0)


def alive_lanes(step, near):
    lane = lax.broadcasted_iota(jnp.int32, (1, 256), 1)
    out = jnp.zeros((1, 256), f32)
    for i in range(quad):
        live = (near[(step * quad + i) * 27 + 13] != zero_row).astype(f32)
        out = jnp.where(lane // 64 == i, live, out)
    return out


def quad_cotangent(cot, at, t, low):
    even, odd = [], []
    for pair in range(2):
        e, o = to_pair(
            (
                cot[at + 2 * pair, :, t * 128 : t * 128 + 128],
                cot[at + 2 * pair + 1, :, t * 128 : t * 128 + 128],
            ),
            low,
        )
        even.append(e)
        odd.append(o)
    return (
        jnp.concatenate(even, axis=1).astype(f32),
        jnp.concatenate(odd, axis=1).astype(f32),
    )


def from_pair(ref, at, even, odd, t, low):
    for pair in range(2):
        e = even[:, pair * 128 : pair * 128 + 128]
        o = odd[:, pair * 128 : pair * 128 + 128]
        ref[at + 2 * pair, :, t * 128 : t * 128 + 128] = jnp.where(low, e, roll(o, 64))
        ref[at + 2 * pair + 1, :, t * 128 : t * 128 + 128] = jnp.where(low, roll(e, 64), o)


def forward_kernel(
    near, lists, hidden, rxm, rxp, rym, ryp, cot, taps, elow, ehigh, ylow, yhigh, shift,
    block_out, grad, term, xm, xp, ym, yp,
    table, weight, wide, kinds, turned, stacks, total, term_wide,
):
    step = pl.program_id(0)

    def build(index, slot):
        build_stack(index, near, table, shift, kinds[slot], turned[slot], stacks[slot])

    @pl.when(step == 0)
    def _():
        banded(taps, weight)
        fill_table(table, hidden, rxm, rxp, rym, ryp, elow, ehigh)
        total[...] = jnp.zeros_like(total)
        build(0, 0)

    low = lane_id(channels) < 64

    def process(index, slot):
        stack = stacks[slot]
        pre_all = convolve(weight, stack)
        live = alive_lanes(index, near)
        grad_pair = []
        for t in range(4):
            cots = quad_cotangent(cot, slot * quad, t, low)
            mixed, grads = [], []
            for p in range(2):
                x = 2 * t + p
                pre = pre_all[x * 32 : x * 32 + 32]
                row = (x + 1) * band + 4 * channels
                here = stack[row : row + channels, :].astype(f32)
                sigma = 0.5 * jnp.tanh(0.5 * pre) + 0.5
                mixed.append(((here + pre * sigma) * live).astype(bf16))
                grads.append((cots[p] * (sigma * (1.0 + pre * (1.0 - sigma))) * live).astype(bf16))
            from_pair(block_out, slot * quad, mixed[0], mixed[1], t, low)
            from_pair(grad, index * quad, grads[0], grads[1], t, low)
            grad_pair += grads
        grad_all = jnp.concatenate(grad_pair, axis=0)
        for x in range(10):
            total[x * band : x * band + band] += lax.dot_general(
                stack[x * band : x * band + band],
                grad_all,
                (((1,), (1,)), ((), ())),
                preferred_element_type=f32,
            )

    build(2 * step + 1, 1)
    process(2 * step, 0)
    build(jnp.minimum(2 * step + 2, steps - 1), 0)
    process(2 * step + 1, 1)

    @pl.when(step == steps // 2 - 1)
    def _():
        emit_faces(lists, grad, ylow, yhigh, xm, xp, ym, yp, wide)
        acc = total[0 : 3 * band, 0:32]
        for x in range(1, 8):
            acc = acc + total[x * band : x * band + 3 * band, x * 32 : x * 32 + 32]
        term_wide[...] = jnp.zeros((1024, 128), f32)
        term_wide[0 : 3 * band, 0:32] = acc
        across = term_wide[...].T
        for j in range(4):
            for half in range(2):
                at_lane = j * 256 + half * 128
                term[j * 32 : j * 32 + 32, half, :] = across[0:32, at_lane : at_lane + 128]


def backward_kernel(
    near, child, grad, rxm, rxp, rym, ryp, cot, taps, elow, ehigh, pool, shift, terms,
    fine_grad, back,
    table, weight, kinds, turned, stacks, octants,
):
    step = pl.program_id(0)

    def build(index, slot):
        build_stack(index, near, table, shift, kinds[slot], turned[slot], stacks[slot])

    @pl.when(step == 0)
    def _():
        banded(taps, weight)
        fill_table(table, grad, rxm, rxp, rym, ryp, elow, ehigh)
        build(0, 0)
        rest = jnp.sum(terms[...], axis=0)
        rows = []
        for i in range(3):
            part = rest.astype(bf16)
            rest = rest - part.astype(f32)
            rows += [part.astype(f32)]
        rows += [jnp.zeros((2, 128), f32)]
        tail = jnp.concatenate(rows, axis=0).astype(bf16)
        clear = jnp.zeros((16, 128), bf16)

        def body(i, carry):
            for j in range(8):
                back[i * 8 + j, 0:16, :] = clear
                back[i * 8 + j, 16:24, :] = tail
            return carry

        lax.fori_loop(0, 16, body, 0)

    low = lane_id(channels) < 64
    low16 = lane_id(16) < 64

    def process(index, slot):
        conv = convolve(weight, stacks[slot])
        live = alive_lanes(index, near)
        sums = []
        for t in range(4):
            cots = quad_cotangent(cot, slot * quad, t, low)
            full = [
                (cots[p] + conv[(2 * t + p) * 32 : (2 * t + p) * 32 + 32]) * live
                for p in range(2)
            ]
            from_pair(fine_grad, slot * quad, full[0].astype(bf16), full[1].astype(bf16), t, low)
            both = full[0] + full[1]
            for pair in range(2):
                v = both[:, pair * 128 : pair * 128 + 128]
                v = v + roll(v, -1)
                v = v + roll(v, -8)
                sums.append(v.astype(bf16))
        rows = pl.ds(pl.multiple_of(index * channels, channels), channels)
        for i in range(8):
            octants[rows, i * 128 : i * 128 + 128] = sums[i]

    build(2 * step + 1, 1)
    process(2 * step, 0)
    process(2 * step + 1, 1)
    build(jnp.minimum(2 * step + 2, steps - 1), 0)

    @pl.when(step == steps // 2 - 1)
    def _():
        pooled = jnp.dot(octants[...], pool[...], preferred_element_type=f32).astype(bf16)
        for s in range(capacity):
            row = s // quad * channels
            at_lane = (s % quad) // 2 * 128
            tile = pooled[row : row + channels, at_lane : at_lane + 128]
            if s % 2 == 0:
                packed = jnp.where(low16, tile[:16], roll(tile[16:], 64))
            else:
                packed = jnp.where(low16, roll(tile[:16], 64), tile[16:])
            back[child[s], 0:16, :] = packed


def last_kernel(send, returned, perm, coarse_grad, weight_grad, tab, parts):
    low = lane_id(16) < 64
    tab[...] = jnp.zeros_like(tab)

    def body(i, carry):
        for j in range(8):
            d = i * 8 + j
            target = send[d]

            @pl.when(target >= 0)
            def _():
                tab[target] = returned[d, 0:16, :]

        return carry

    lax.fori_loop(0, 16, body, 0)
    rows = []
    for i in range(8):
        tops, bottoms = [], []
        for g in range(4):
            a, b = tab[i * 8 + 2 * g], tab[i * 8 + 2 * g + 1]
            tops.append(jnp.where(low, a, roll(b, 64)))
            bottoms.append(jnp.where(low, roll(a, 64), b))
        rows.append(jnp.concatenate(tops, axis=1))
        rows.append(jnp.concatenate(bottoms, axis=1))
    spread = jnp.dot(jnp.concatenate(rows, axis=0), perm[...], preferred_element_type=f32)
    coarse_grad[...] = spread.astype(bf16).reshape(8, 32, 512)
    parts[...] = returned[:, 16:24, :].astype(f32)
    for half in range(2):
        total = parts[:, half, :] + parts[:, half + 2, :] + parts[:, half + 4, :]
        for j in range(4):
            for i in range(4):
                k = j * 8 + half * 4 + i
                if k < 27:
                    weight_grad[k] = total[j * 32 : j * 32 + 32, i * 32 : i * 32 + 32]


def shape(dims, kind=bf16):
    return jax.ShapeDtypeStruct(dims, kind)


def ranks(flags):
    before = (jnp.arange(capacity)[:, None] < jnp.arange(capacity)[None, :]).astype(bf16)
    return jnp.dot(flags.astype(bf16), before, preferred_element_type=f32).astype(jnp.int32)


def indices(adjacency):
    table_id = jnp.arange(9 * capacity, dtype=jnp.int32)
    hits = adjacency[:, :, None] == table_id
    rank = ranks(hits.any(axis=(0, 1)).reshape(9, capacity)).reshape(-1)
    row_base = jnp.asarray(np.repeat(np.array(place_base), capacity), jnp.int32)
    own = (table_id // capacity) == 4
    row_of = jnp.where(own, table_id % capacity, row_base + rank)
    near = jnp.sum(jnp.where(hits, row_of, 0), axis=2)
    near = jnp.where(adjacency < 0, zero_row, near)
    place = jnp.where(adjacency < 0, -1, adjacency // capacity)
    need = (place[None, :, :] == jnp.arange(9)[:, None, None]).any(axis=2)
    order = ranks(need)
    slot = jnp.arange(capacity, dtype=jnp.int32)
    pick = need[:, None, :] & (order[:, None, :] == jnp.arange(face_n)[None, :, None])
    chosen = jnp.sum(jnp.where(pick, slot, 0), axis=2)
    lists = jnp.concatenate(
        [
            chosen[1], chosen[0, :corner_n], chosen[2, :corner_n],
            chosen[7], chosen[6, :corner_n], chosen[8, :corner_n],
            chosen[3], chosen[5],
        ]
    )
    return near.reshape(-1).astype(jnp.int32), lists.astype(jnp.int32)


def moved(value, shift_x, shift_y):
    count_x, count_y = lax.axis_size("gx"), lax.axis_size("gy")
    pairs = [
        (i * count_y + j, (i + shift_x) * count_y + j + shift_y)
        for i in range(count_x)
        for j in range(count_y)
        if 0 <= i + shift_x < count_x and 0 <= j + shift_y < count_y
    ]
    return lax.ppermute(value, axes, pairs)


def halo(xm, xp, ym, yp):
    from_xm = moved(xp, 1, 0)
    from_xp = moved(xm, -1, 0)
    mid = face_n + corner_n
    up = jnp.concatenate([yp, from_xm[mid:], from_xp[mid:]], axis=0)
    down = jnp.concatenate([ym, from_xm[face_n:mid], from_xp[face_n:mid]], axis=0)
    from_ym = moved(up, 0, 1)
    from_yp = moved(down, 0, -1)
    return from_xm, from_xp, from_ym, from_yp


def exchange(value):
    return lax.all_to_all(value, axes, split_axis=0, concat_axis=0, tiled=True)


def whole(dims):
    return pl.BlockSpec(dims, lambda i: (0,) * len(dims))


def on_device(fine, coarse, weight, cotangent, adjacency, send_list, child_src):
    devices = lax.axis_size("gx") * lax.axis_size("gy")
    send = send_list.reshape(-1)
    perm = const(octant_matrix())
    perm_t = const(octant_matrix().T)
    y_low, y_high = y_face_matrix(0), y_face_matrix(7)
    ylow, yhigh = const(y_low), const(y_high)
    elow, ehigh = const(y_low.T), const(y_high.T)
    up = const(upsample_matrix())
    pool = const(pool_matrix())
    shift = const(shift_matrix())
    packed = (16, 128)
    side = shape((side_n,) + packed)
    face = shape((face_n,) + packed)

    outgoing = pl.pallas_call(
        octant_kernel,
        out_shape=shape((devices,) + packed),
        in_specs=[smem, vmem, vmem],
        out_specs=vmem,
        scratch_shapes=[pltpu.VMEM((64,) + packed, bf16)],
        compiler_params=params(),
        name="octants",
    )(send, coarse, perm)
    incoming = exchange(outgoing)

    near, lists = indices(adjacency)
    alive = (adjacency[:, 13] >= 0).astype(jnp.int32)
    sender = jnp.arange(devices, dtype=jnp.int32)
    unused = jnp.where((child_src[:, None] == sender).any(axis=0), devices, sender).min()
    back_to = jnp.where(child_src < 0, unused, child_src)
    taps = weight.transpose(1, 0, 2).reshape(channels, 27 * channels)
    back_taps = weight[::-1].transpose(2, 0, 1).reshape(channels, 27 * channels)

    part = pl.BlockSpec((16, channels, 512), lambda i: (i, 0, 0))
    hidden, xm, xp, ym, yp = pl.pallas_call(
        hidden_kernel,
        grid=(capacity // 16,),
        out_shape=(shape((capacity, channels, 512)), side, side, face, face),
        in_specs=[smem, smem, smem, whole((devices,) + packed), part]
        + [whole((128, 1024))]
        + [whole((1024, 128))] * 2,
        out_specs=(part,) + tuple(whole((n,) + packed) for n in (side_n, side_n, face_n, face_n)),
        scratch_shapes=[
            pltpu.VMEM((face_n * 16, 1024), bf16),
            pltpu.VMEM((capacity, channels, 512), bf16),
        ],
        compiler_params=params(),
        name="hidden",
    )(child_src, alive, lists, incoming, fine, up, ylow, yhigh)
    near_h = halo(xm, xp, ym, yp)

    bricks = whole((capacity, channels, 512))
    sides = [whole((side_n,) + packed)] * 4
    per_step = pl.BlockSpec((2 * quad, channels, 512), lambda i: (i, 0, 0))
    table = pltpu.VMEM((table_rows, channels, 512), bf16)
    wide = pltpu.VMEM((face_n * 16, 1024), bf16)
    banded_weight = pltpu.VMEM((256, depth), bf16)
    work = [
        [pltpu.VMEM((1280, 256), bf16)] * 2,
        [pltpu.VMEM((1280, 256), bf16)] * 2,
        [pltpu.VMEM((depth, 256), bf16)] * 2,
    ]
    block_out, grad, term, gxm, gxp, gym, gyp = pl.pallas_call(
        forward_kernel,
        grid=(steps // 2,),
        out_shape=(
            shape((capacity, channels, 512)),
            shape((capacity, channels, 512)),
            shape((devices, 2, 128), f32),
            side, side, face, face,
        ),
        in_specs=[smem, smem, bricks]
        + sides
        + [per_step, whole((channels, 27 * channels))]
        + [whole((128, 1024))] * 2
        + [whole((1024, 128))] * 2
        + [whole((256, 256))],
        out_specs=(per_step, bricks, whole((devices, 2, 128)))
        + tuple(whole((n,) + packed) for n in (side_n, side_n, face_n, face_n)),
        scratch_shapes=[table, banded_weight, wide]
        + work
        + [pltpu.VMEM((depth, 256), f32), pltpu.VMEM((1024, 128), f32)],
        compiler_params=params(),
        name="forward",
    )(near, lists, hidden, *near_h, cotangent, taps, elow, ehigh, ylow, yhigh, shift)
    near_g = halo(gxm, gxp, gym, gyp)
    terms = exchange(term)

    fine_grad, back = pl.pallas_call(
        backward_kernel,
        grid=(steps // 2,),
        out_shape=(shape((capacity, channels, 512)), shape((devices, 24, 128))),
        in_specs=[smem, smem, bricks]
        + sides
        + [per_step, whole((channels, 27 * channels)), whole((128, 1024)), whole((128, 1024))]
        + [whole((1024, 256)), whole((256, 256)), whole((devices, 2, 128))],
        out_specs=(per_step, whole((devices, 24, 128))),
        scratch_shapes=[table, banded_weight] + work + [pltpu.VMEM((steps * channels, 1024), bf16)],
        compiler_params=params(),
        name="backward",
    )(near, back_to, grad, *near_g, cotangent, back_taps, elow, ehigh, pool, shift, terms)
    returned = exchange(back)

    coarse_grad, weight_grad = pl.pallas_call(
        last_kernel,
        out_shape=(shape((8, channels, 512)), shape((27, channels, channels), f32)),
        in_specs=[smem, vmem, vmem],
        out_specs=(vmem, vmem),
        scratch_shapes=[pltpu.VMEM((64,) + packed, bf16), pltpu.VMEM((devices, 8, 128), f32)],
        compiler_params=params(),
        name="coarse",
    )(send, returned, perm_t)
    return block_out, fine_grad, coarse_grad, weight_grad


def solution(mesh):
    return jax.shard_map(
        on_device,
        mesh=mesh,
        in_specs=(
            P(axes, None, None),
            P(axes, None, None),
            P(),
            P(axes, None, None),
            P(axes, None),
            P(axes, None),
            P(axes),
        ),
        out_specs=(
            P(axes, None, None),
            P(axes, None, None),
            P(axes, None, None),
            P(),
        ),
        check_vma=False,
    )
```

```python
import jax
import jax.numpy as jnp
import numpy as np
from jax import lax
from jax.experimental import pallas as pl
from jax.experimental.pallas import tpu as pltpu
from jax.sharding import PartitionSpec as P

axes = ("gx", "gy")
channels = 32
capacity = 64
quad = 4
steps = capacity // quad
band = 9 * channels
depth = 10 * band
face_n = 16
corner_n = 4
side_n = face_n + 2 * corner_n
base_xm = capacity
base_xp = base_xm + face_n
base_ym = base_xp + face_n
base_yp = base_ym + side_n
zero_row = base_yp + side_n
table_rows = zero_row + 1
place_base = (
    base_ym + face_n,
    base_xm,
    base_yp + face_n,
    base_ym,
    0,
    base_yp,
    base_ym + face_n + corner_n,
    base_xp,
    base_yp + face_n + corner_n,
)
vmem = pl.BlockSpec(memory_space=pltpu.VMEM)
smem = pl.BlockSpec(memory_space=pltpu.SMEM)
bf16 = jnp.bfloat16
f32 = jnp.float32


def params():
    return pltpu.CompilerParams(vmem_limit_bytes=60 * 1024 * 1024)


def octant_matrix():
    out = np.zeros((512, 512), np.float32)
    for o in range(8):
        a, b, c = o // 4, o // 2 % 2, o % 2
        for v in range(64):
            x, y, z = v // 16, v // 4 % 4, v % 4
            out[(4 * a + x) * 64 + (4 * b + y) * 8 + 4 * c + z, o * 64 + v] = 1
    return out


def upsample_matrix():
    out = np.zeros((64, 512), np.float32)
    for p in range(512):
        x, y, z = p // 64, p // 8 % 8, p % 8
        out[(x // 2) * 16 + (y // 2) * 4 + z // 2, p] = 1
    wide = np.zeros((128, 1024), np.float32)
    wide[:64, :512] = out
    wide[64:, 512:] = out
    return wide


def y_face_matrix(y):
    out = np.zeros((512, 64), np.float32)
    for x in range(8):
        for z in range(8):
            out[x * 64 + y * 8 + z, x * 8 + z] = 1
    wide = np.zeros((1024, 128), np.float32)
    wide[:512, :64] = out
    wide[512:, 64:] = out
    return wide


def pool_matrix():
    out = np.zeros((4, 2, 128, 256), np.float32)
    for t in range(4):
        for b in range(4):
            for y in range(0, 8, 2):
                for z in range(0, 8, 2):
                    out[t, b // 2, (b % 2) * 64 + y * 8 + z, b * 64 + t * 16 + (y // 2) * 4 + z // 2] = 1
    return out.reshape(1024, 256)


def const(values):
    return jnp.asarray(values, dtype=bf16)


def lane_id(rows):
    return lax.broadcasted_iota(jnp.int32, (rows, 128), 1)


def roll(v, shift):
    return pltpu.roll(v, shift % 128, 1)


def octant_kernel(send, coarse, perm, out, tab):
    low = lane_id(16) < 64
    y = jnp.dot(coarse[...].reshape(256, 512), perm[...], preferred_element_type=f32).astype(bf16)
    for i in range(8):
        for g in range(4):
            part = y[i * 32 : i * 32 + 32, g * 128 : g * 128 + 128]
            tab[i * 8 + 2 * g] = jnp.where(low, part[:16], roll(part[16:], 64))
            tab[i * 8 + 2 * g + 1] = jnp.where(low, roll(part[:16], 64), part[16:])

    def body(i, carry):
        for j in range(8):
            d = i * 8 + j
            out[d] = tab[jnp.maximum(send[d], 0)]
        return carry

    lax.fori_loop(0, 16, body, 0)


def emit_faces(lists, bricks, ylow, yhigh, out_xm, out_xp, out_ym, out_yp, wide):
    low = lane_id(16) < 64
    for r in range(side_n):
        s = lists[r]
        out_xm[r] = jnp.where(low, bricks[s, 0:16, 0:128], roll(bricks[s, 16:32, 0:128], 64))
        s = lists[side_n + r]
        out_xp[r] = jnp.where(low, roll(bricks[s, 0:16, 384:512], 64), bricks[s, 16:32, 384:512])
    for side, (matrix, out) in enumerate(((ylow, out_ym), (yhigh, out_yp))):
        for r in range(face_n):
            s = lists[2 * side_n + side * face_n + r]
            wide[r * 16 : r * 16 + 16, 0:512] = bricks[s, 0:16, :]
            wide[r * 16 : r * 16 + 16, 512:1024] = bricks[s, 16:32, :]
        out[...] = (
            jnp.dot(wide[...], matrix[...], preferred_element_type=f32)
            .astype(bf16)
            .reshape(face_n, 16, 128)
        )


def hidden_kernel(
    child, alive, lists, incoming, fine, up, ylow, yhigh, hidden, xm, xp, ym, yp, wide, full
):
    step = pl.program_id(0)
    rows = []
    for j in range(16):
        rows.append(incoming[jnp.maximum(child[step * 16 + j], 0)])
    big = jnp.dot(jnp.concatenate(rows, axis=0), up[...], preferred_element_type=f32)
    for j in range(16):
        s = step * 16 + j
        live = (alive[s] > 0).astype(f32)
        for h in range(2):
            total = fine[j, h * 16 : h * 16 + 16, :].astype(f32) + big[
                j * 16 : j * 16 + 16, h * 512 : h * 512 + 512
            ]
            value = (total * live).astype(bf16)
            hidden[j, h * 16 : h * 16 + 16, :] = value
            full[s, h * 16 : h * 16 + 16, :] = value

    @pl.when(step == pl.num_programs(0) - 1)
    def _():
        emit_faces(lists, full, ylow, yhigh, xm, xp, ym, yp, wide)


def fill_table(table, own, rxm, rxp, rym, ryp, elow, ehigh):
    def copy(i, carry):
        for j in range(8):
            table[i * 8 + j] = own[i * 8 + j]
        return carry

    lax.fori_loop(0, capacity // 8, copy, 0)
    for row, source, at in (
        [(base_xm + r, rxm, r) for r in range(face_n)]
        + [(base_ym + face_n + r, rym, face_n + r) for r in range(corner_n)]
        + [(base_yp + face_n + r, ryp, face_n + r) for r in range(corner_n)]
    ):
        table[row, 0:16, 384:512] = roll(source[at], 64)
        table[row, 16:32, 384:512] = source[at]
    for row, source, at in (
        [(base_xp + r, rxp, r) for r in range(face_n)]
        + [(base_ym + face_n + corner_n + r, rym, face_n + corner_n + r) for r in range(corner_n)]
        + [(base_yp + face_n + corner_n + r, ryp, face_n + corner_n + r) for r in range(corner_n)]
    ):
        table[row, 0:16, 0:128] = source[at]
        table[row, 16:32, 0:128] = roll(source[at], 64)
    for base, source, matrix in ((base_ym, rym, ehigh), (base_yp, ryp, elow)):
        big = jnp.dot(
            source[0:face_n].reshape(face_n * 16, 128), matrix[...], preferred_element_type=f32
        ).astype(bf16)
        for r in range(face_n):
            table[base + r, 0:16, :] = big[r * 16 : r * 16 + 16, 0:512]
            table[base + r, 16:32, :] = big[r * 16 : r * 16 + 16, 512:1024]
    table[zero_row] = jnp.zeros((channels, 512), bf16)


def to_pair(even_odd, low):
    first, second = even_odd
    return (
        jnp.where(low, first, roll(second, 64)),
        jnp.where(low, roll(first, 64), second),
    )


def shift_matrix():
    out = np.zeros((256, 256), np.float32)
    for lane in range(128):
        z = lane % 8
        out[lane - 1 if z > 0 else 128 + lane + 7, lane] = 1
        out[lane + 1 if z < 7 else 128 + lane - 7, 128 + lane] = 1
    return out


def build_stack(index, near, table, shift, kinds, turned, stack):
    lane = lane_id(channels)
    inner = lane & 63
    low = lane < 64
    y_first, y_last = inner < 8, inner >= 56
    z_last = (lane & 7) == 7

    def sources(brick, off_x, tile):
        def at(off_y, off_z):
            row = near[brick * 27 + (off_x + 1) * 9 + (off_y + 1) * 3 + off_z + 1]
            return table[row, :, tile * 128 : tile * 128 + 128]

        return (
            at(0, 0),
            jnp.where(z_last, at(0, -1), at(0, 1)),
            jnp.where(y_last, at(-1, 0), at(1, 0)),
            jnp.where(
                y_last,
                jnp.where(z_last, at(-1, -1), at(-1, 1)),
                jnp.where(z_last, at(1, -1), at(1, 1)),
            ),
        )

    for pair in range(2):
        b0 = index * quad + 2 * pair
        for off_x, tile in ((-1, 3), (0, 0), (0, 1), (0, 2), (0, 3), (1, 0)):
            first = sources(b0, off_x, tile)
            second = sources(b0 + 1, off_x, tile)
            for kind in range(4):
                swap = kind >= 2
                even, odd = to_pair(
                    (second[kind], first[kind]) if swap else (first[kind], second[kind]), low
                )
                base = (2 * pair + kind // 2) * 320
                at_lane = (kind % 2) * 128
                if off_x <= 0:
                    row = base + (0 if off_x < 0 else 2 + 2 * tile) * channels
                    kinds[row : row + channels, at_lane : at_lane + 128] = odd
                if off_x >= 0:
                    row = base + (9 if off_x > 0 else 1 + 2 * tile) * channels
                    kinds[row : row + channels, at_lane : at_lane + 128] = even
    turned[...] = jnp.dot(kinds[...], shift[...], preferred_element_type=f32).astype(bf16)
    for pair in range(2):
        for plane in range(10):
            own_row = 2 * pair * 320 + plane * channels
            far_row = own_row + 320
            for k in range(3):
                source, at_lane = ((turned, 0), (kinds, 0), (turned, 128))[k]
                own = source[own_row : own_row + channels, at_lane : at_lane + 128]
                far = source[far_row : far_row + channels, at_lane : at_lane + 128]
                trio = (
                    roll(jnp.where(y_last, far, own), 8),
                    own,
                    roll(jnp.where(y_first, far, own), -8),
                )
                for j in range(3):
                    row = plane * band + (j * 3 + k) * channels
                    stack[row : row + channels, pair * 128 : pair * 128 + 128] = trio[j]


def banded(taps, weight):
    weight[...] = jnp.zeros_like(weight)
    for x in range(8):
        weight[x * 32 : x * 32 + 32, x * band : x * band + 3 * band] = taps[...]


def convolve(weight, stack):
    halves = []
    for h in range(2):
        seen = slice(h * 4 * band, h * 4 * band + 6 * band)
        halves.append(
            jnp.dot(weight[h * 128 : h * 128 + 128, seen], stack[seen], preferred_element_type=f32)
        )
    return jnp.concatenate(halves, axis=0)


def alive_lanes(step, near):
    lane = lax.broadcasted_iota(jnp.int32, (1, 256), 1)
    out = jnp.zeros((1, 256), f32)
    for i in range(quad):
        live = (near[(step * quad + i) * 27 + 13] != zero_row).astype(f32)
        out = jnp.where(lane // 64 == i, live, out)
    return out


def quad_cotangent(cot, at, t, low):
    even, odd = [], []
    for pair in range(2):
        e, o = to_pair(
            (
                cot[at + 2 * pair, :, t * 128 : t * 128 + 128],
                cot[at + 2 * pair + 1, :, t * 128 : t * 128 + 128],
            ),
            low,
        )
        even.append(e)
        odd.append(o)
    return (
        jnp.concatenate(even, axis=1).astype(f32),
        jnp.concatenate(odd, axis=1).astype(f32),
    )


def from_pair(ref, at, even, odd, t, low):
    for pair in range(2):
        e = even[:, pair * 128 : pair * 128 + 128]
        o = odd[:, pair * 128 : pair * 128 + 128]
        ref[at + 2 * pair, :, t * 128 : t * 128 + 128] = jnp.where(low, e, roll(o, 64))
        ref[at + 2 * pair + 1, :, t * 128 : t * 128 + 128] = jnp.where(low, roll(e, 64), o)


def forward_kernel(
    near, lists, hidden, rxm, rxp, rym, ryp, cot, taps, elow, ehigh, ylow, yhigh, shift,
    block_out, grad, term, xm, xp, ym, yp,
    table, weight, wide, kinds, turned, stacks, total, term_wide,
):
    step = pl.program_id(0)

    def build(index, slot):
        build_stack(index, near, table, shift, kinds[slot], turned[slot], stacks[slot])

    @pl.when(step == 0)
    def _():
        banded(taps, weight)
        fill_table(table, hidden, rxm, rxp, rym, ryp, elow, ehigh)
        total[...] = jnp.zeros_like(total)
        build(0, 0)

    low = lane_id(channels) < 64

    def process(index, slot):
        stack = stacks[slot]
        pre_all = convolve(weight, stack)
        live = alive_lanes(index, near)
        grad_pair = []
        for t in range(4):
            cots = quad_cotangent(cot, slot * quad, t, low)
            mixed, grads = [], []
            for p in range(2):
                x = 2 * t + p
                pre = pre_all[x * 32 : x * 32 + 32]
                row = (x + 1) * band + 4 * channels
                here = stack[row : row + channels, :].astype(f32)
                sigma = 0.5 * jnp.tanh(0.5 * pre) + 0.5
                mixed.append(((here + pre * sigma) * live).astype(bf16))
                grads.append((cots[p] * (sigma * (1.0 + pre * (1.0 - sigma))) * live).astype(bf16))
            from_pair(block_out, slot * quad, mixed[0], mixed[1], t, low)
            from_pair(grad, index * quad, grads[0], grads[1], t, low)
            grad_pair += grads
        grad_all = jnp.concatenate(grad_pair, axis=0)
        for x in range(10):
            total[x * band : x * band + band] += lax.dot_general(
                stack[x * band : x * band + band],
                grad_all,
                (((1,), (1,)), ((), ())),
                preferred_element_type=f32,
            )

    build(2 * step + 1, 1)
    process(2 * step, 0)
    build(jnp.minimum(2 * step + 2, steps - 1), 0)
    process(2 * step + 1, 1)

    @pl.when(step == steps // 2 - 1)
    def _():
        emit_faces(lists, grad, ylow, yhigh, xm, xp, ym, yp, wide)
        acc = total[0 : 3 * band, 0:32]
        for x in range(1, 8):
            acc = acc + total[x * band : x * band + 3 * band, x * 32 : x * 32 + 32]
        term_wide[...] = jnp.zeros((1024, 128), f32)
        term_wide[0 : 3 * band, 0:32] = acc
        across = term_wide[...].T
        for j in range(4):
            for half in range(2):
                at_lane = j * 256 + half * 128
                term[j * 32 : j * 32 + 32, half, :] = across[0:32, at_lane : at_lane + 128]


def backward_kernel(
    near, child, grad, rxm, rxp, rym, ryp, cot, taps, elow, ehigh, pool, shift, terms,
    fine_grad, back,
    table, weight, kinds, turned, stacks, octants,
):
    step = pl.program_id(0)

    def build(index, slot):
        build_stack(index, near, table, shift, kinds[slot], turned[slot], stacks[slot])

    @pl.when(step == 0)
    def _():
        banded(taps, weight)
        fill_table(table, grad, rxm, rxp, rym, ryp, elow, ehigh)
        build(0, 0)
        rest = jnp.sum(terms[...], axis=0)
        rows = []
        for i in range(3):
            part = rest.astype(bf16)
            rest = rest - part.astype(f32)
            rows += [part.astype(f32)]
        rows += [jnp.zeros((2, 128), f32)]
        tail = jnp.concatenate(rows, axis=0).astype(bf16)
        clear = jnp.zeros((16, 128), bf16)

        def body(i, carry):
            for j in range(8):
                back[i * 8 + j, 0:16, :] = clear
                back[i * 8 + j, 16:24, :] = tail
            return carry

        lax.fori_loop(0, 16, body, 0)

    low = lane_id(channels) < 64
    low16 = lane_id(16) < 64

    def process(index, slot):
        conv = convolve(weight, stacks[slot])
        live = alive_lanes(index, near)
        sums = []
        for t in range(4):
            cots = quad_cotangent(cot, slot * quad, t, low)
            full = [
                (cots[p] + conv[(2 * t + p) * 32 : (2 * t + p) * 32 + 32]) * live
                for p in range(2)
            ]
            from_pair(fine_grad, slot * quad, full[0].astype(bf16), full[1].astype(bf16), t, low)
            both = full[0] + full[1]
            for pair in range(2):
                v = both[:, pair * 128 : pair * 128 + 128]
                v = v + roll(v, -1)
                v = v + roll(v, -8)
                sums.append(v.astype(bf16))
        rows = pl.ds(pl.multiple_of(index * channels, channels), channels)
        for i in range(8):
            octants[rows, i * 128 : i * 128 + 128] = sums[i]

    build(2 * step + 1, 1)
    process(2 * step, 0)
    process(2 * step + 1, 1)
    build(jnp.minimum(2 * step + 2, steps - 1), 0)

    @pl.when(step == steps // 2 - 1)
    def _():
        pooled = jnp.dot(octants[...], pool[...], preferred_element_type=f32).astype(bf16)
        for s in range(capacity):
            row = s // quad * channels
            at_lane = (s % quad) // 2 * 128
            tile = pooled[row : row + channels, at_lane : at_lane + 128]
            if s % 2 == 0:
                packed = jnp.where(low16, tile[:16], roll(tile[16:], 64))
            else:
                packed = jnp.where(low16, roll(tile[:16], 64), tile[16:])
            back[child[s], 0:16, :] = packed


def last_kernel(send, returned, perm, coarse_grad, weight_grad, tab, parts):
    low = lane_id(16) < 64
    tab[...] = jnp.zeros_like(tab)

    def body(i, carry):
        for j in range(8):
            d = i * 8 + j
            target = send[d]

            @pl.when(target >= 0)
            def _():
                tab[target] = returned[d, 0:16, :]

        return carry

    lax.fori_loop(0, 16, body, 0)
    rows = []
    for i in range(8):
        tops, bottoms = [], []
        for g in range(4):
            a, b = tab[i * 8 + 2 * g], tab[i * 8 + 2 * g + 1]
            tops.append(jnp.where(low, a, roll(b, 64)))
            bottoms.append(jnp.where(low, roll(a, 64), b))
        rows.append(jnp.concatenate(tops, axis=1))
        rows.append(jnp.concatenate(bottoms, axis=1))
    spread = jnp.dot(jnp.concatenate(rows, axis=0), perm[...], preferred_element_type=f32)
    coarse_grad[...] = spread.astype(bf16).reshape(8, 32, 512)
    parts[...] = returned[:, 16:24, :].astype(f32)
    for half in range(2):
        total = parts[:, half, :] + parts[:, half + 2, :] + parts[:, half + 4, :]
        for j in range(4):
            for i in range(4):
                k = j * 8 + half * 4 + i
                if k < 27:
                    weight_grad[k] = total[j * 32 : j * 32 + 32, i * 32 : i * 32 + 32]


def shape(dims, kind=bf16):
    return jax.ShapeDtypeStruct(dims, kind)


def ranks(flags):
    before = (jnp.arange(capacity)[:, None] < jnp.arange(capacity)[None, :]).astype(bf16)
    return jnp.dot(flags.astype(bf16), before, preferred_element_type=f32).astype(jnp.int32)


def indices(adjacency):
    table_id = jnp.arange(9 * capacity, dtype=jnp.int32)
    hits = adjacency[:, :, None] == table_id
    rank = ranks(hits.any(axis=(0, 1)).reshape(9, capacity)).reshape(-1)
    row_base = jnp.asarray(np.repeat(np.array(place_base), capacity), jnp.int32)
    own = (table_id // capacity) == 4
    row_of = jnp.where(own, table_id % capacity, row_base + rank)
    near = jnp.sum(jnp.where(hits, row_of, 0), axis=2)
    near = jnp.where(adjacency < 0, zero_row, near)
    place = jnp.where(adjacency < 0, -1, adjacency // capacity)
    need = (place[None, :, :] == jnp.arange(9)[:, None, None]).any(axis=2)
    order = ranks(need)
    slot = jnp.arange(capacity, dtype=jnp.int32)
    pick = need[:, None, :] & (order[:, None, :] == jnp.arange(face_n)[None, :, None])
    chosen = jnp.sum(jnp.where(pick, slot, 0), axis=2)
    lists = jnp.concatenate(
        [
            chosen[1], chosen[0, :corner_n], chosen[2, :corner_n],
            chosen[7], chosen[6, :corner_n], chosen[8, :corner_n],
            chosen[3], chosen[5],
        ]
    )
    return near.reshape(-1).astype(jnp.int32), lists.astype(jnp.int32)


def moved(value, shift_x, shift_y):
    count_x, count_y = lax.axis_size("gx"), lax.axis_size("gy")
    pairs = [
        (i * count_y + j, (i + shift_x) * count_y + j + shift_y)
        for i in range(count_x)
        for j in range(count_y)
        if 0 <= i + shift_x < count_x and 0 <= j + shift_y < count_y
    ]
    return lax.ppermute(value, axes, pairs)


def join(ym, yp, from_xm, from_xp, down, up):
    for out, plane, at in ((down, ym, face_n), (up, yp, face_n + corner_n)):
        out[0:face_n] = plane[...]
        out[face_n : face_n + corner_n] = from_xm[at : at + corner_n]
        out[face_n + corner_n : side_n] = from_xp[at : at + corner_n]


def join_term_kernel(ym, yp, from_xm, from_xp, term, down, up, passed):
    join(ym, yp, from_xm, from_xp, down, up)
    passed[...] = term[...]


def halo(xm, xp, ym, yp, term=None):
    from_xm = moved(xp, 1, 0)
    from_xp = moved(xm, -1, 0)
    operands = (ym, yp, from_xm, from_xp) + (() if term is None else (term,))
    side = shape((side_n, 16, 128))
    down, up, *passed = pl.pallas_call(
        join if term is None else join_term_kernel,
        out_shape=(side, side) + (() if term is None else (shape(term.shape, f32),)),
        in_specs=[vmem] * len(operands),
        out_specs=(vmem,) * (len(operands) - 2),
        compiler_params=params(),
        name="join",
    )(*operands)
    from_ym = moved(up, 0, 1)
    from_yp = moved(down, 0, -1)
    return [from_xm, from_xp, from_ym, from_yp] + passed


def exchange(value):
    return lax.all_to_all(value, axes, split_axis=0, concat_axis=0, tiled=True)


def whole(dims):
    return pl.BlockSpec(dims, lambda i: (0,) * len(dims))


def on_device(fine, coarse, weight, cotangent, adjacency, send_list, child_src):
    devices = lax.axis_size("gx") * lax.axis_size("gy")
    send = send_list.reshape(-1)
    perm = const(octant_matrix())
    perm_t = const(octant_matrix().T)
    y_low, y_high = y_face_matrix(0), y_face_matrix(7)
    ylow, yhigh = const(y_low), const(y_high)
    elow, ehigh = const(y_low.T), const(y_high.T)
    up = const(upsample_matrix())
    pool = const(pool_matrix())
    shift = const(shift_matrix())
    packed = (16, 128)
    side = shape((side_n,) + packed)
    face = shape((face_n,) + packed)

    outgoing = pl.pallas_call(
        octant_kernel,
        out_shape=shape((devices,) + packed),
        in_specs=[smem, vmem, vmem],
        out_specs=vmem,
        scratch_shapes=[pltpu.VMEM((64,) + packed, bf16)],
        compiler_params=params(),
        name="octants",
    )(send, coarse, perm)
    incoming = exchange(outgoing)

    near, lists = indices(adjacency)
    alive = (adjacency[:, 13] >= 0).astype(jnp.int32)
    sender = jnp.arange(devices, dtype=jnp.int32)
    unused = jnp.where((child_src[:, None] == sender).any(axis=0), devices, sender).min()
    back_to = jnp.where(child_src < 0, unused, child_src)
    taps = weight.transpose(1, 0, 2).reshape(channels, 27 * channels)
    back_taps = weight[::-1].transpose(2, 0, 1).reshape(channels, 27 * channels)

    part = pl.BlockSpec((16, channels, 512), lambda i: (i, 0, 0))
    hidden, xm, xp, ym, yp = pl.pallas_call(
        hidden_kernel,
        grid=(capacity // 16,),
        out_shape=(shape((capacity, channels, 512)), side, side, face, face),
        in_specs=[smem, smem, smem, whole((devices,) + packed), part]
        + [whole((128, 1024))]
        + [whole((1024, 128))] * 2,
        out_specs=(part,) + tuple(whole((n,) + packed) for n in (side_n, side_n, face_n, face_n)),
        scratch_shapes=[
            pltpu.VMEM((face_n * 16, 1024), bf16),
            pltpu.VMEM((capacity, channels, 512), bf16),
        ],
        compiler_params=params(),
        name="hidden",
    )(child_src, alive, lists, incoming, fine, up, ylow, yhigh)
    near_h = halo(xm, xp, ym, yp)

    bricks = whole((capacity, channels, 512))
    sides = [whole((side_n,) + packed)] * 4
    per_step = pl.BlockSpec((2 * quad, channels, 512), lambda i: (i, 0, 0))
    table = pltpu.VMEM((table_rows, channels, 512), bf16)
    wide = pltpu.VMEM((face_n * 16, 1024), bf16)
    banded_weight = pltpu.VMEM((256, depth), bf16)
    work = [
        [pltpu.VMEM((1280, 256), bf16)] * 2,
        [pltpu.VMEM((1280, 256), bf16)] * 2,
        [pltpu.VMEM((depth, 256), bf16)] * 2,
    ]
    block_out, grad, term, gxm, gxp, gym, gyp = pl.pallas_call(
        forward_kernel,
        grid=(steps // 2,),
        out_shape=(
            shape((capacity, channels, 512)),
            shape((capacity, channels, 512)),
            shape((devices, 2, 128), f32),
            side, side, face, face,
        ),
        in_specs=[smem, smem, bricks]
        + sides
        + [per_step, whole((channels, 27 * channels))]
        + [whole((128, 1024))] * 2
        + [whole((1024, 128))] * 2
        + [whole((256, 256))],
        out_specs=(per_step, bricks, whole((devices, 2, 128)))
        + tuple(whole((n,) + packed) for n in (side_n, side_n, face_n, face_n)),
        scratch_shapes=[table, banded_weight, wide]
        + work
        + [pltpu.VMEM((depth, 256), f32), pltpu.VMEM((1024, 128), f32)],
        compiler_params=params(),
        name="forward",
    )(near, lists, hidden, *near_h, cotangent, taps, elow, ehigh, ylow, yhigh, shift)
    *near_g, term = halo(gxm, gxp, gym, gyp, term)
    terms = exchange(term)

    fine_grad, back = pl.pallas_call(
        backward_kernel,
        grid=(steps // 2,),
        out_shape=(shape((capacity, channels, 512)), shape((devices, 24, 128))),
        in_specs=[smem, smem, bricks]
        + sides
        + [per_step, whole((channels, 27 * channels)), whole((128, 1024)), whole((128, 1024))]
        + [whole((1024, 256)), whole((256, 256)), whole((devices, 2, 128))],
        out_specs=(per_step, whole((devices, 24, 128))),
        scratch_shapes=[table, banded_weight] + work + [pltpu.VMEM((steps * channels, 1024), bf16)],
        compiler_params=params(),
        name="backward",
    )(near, back_to, grad, *near_g, cotangent, back_taps, elow, ehigh, pool, shift, terms)
    returned = exchange(back)

    coarse_grad, weight_grad = pl.pallas_call(
        last_kernel,
        out_shape=(shape((8, channels, 512)), shape((27, channels, channels), f32)),
        in_specs=[smem, vmem, vmem],
        out_specs=(vmem, vmem),
        scratch_shapes=[pltpu.VMEM((64,) + packed, bf16), pltpu.VMEM((devices, 8, 128), f32)],
        compiler_params=params(),
        name="coarse",
    )(send, returned, perm_t)
    return block_out, fine_grad, coarse_grad, weight_grad


def solution(mesh):
    return jax.shard_map(
        on_device,
        mesh=mesh,
        in_specs=(
            P(axes, None, None),
            P(axes, None, None),
            P(),
            P(axes, None, None),
            P(axes, None),
            P(axes, None),
            P(axes),
        ),
        out_specs=(
            P(axes, None, None),
            P(axes, None, None),
            P(axes, None, None),
            P(),
        ),
        check_vma=False,
    )
```

```python
import jax
import jax.numpy as jnp
import numpy as np
from jax import lax
from jax.experimental import pallas as pl
from jax.experimental.pallas import tpu as pltpu
from jax.sharding import PartitionSpec as P

axes = ("gx", "gy")
channels = 32
capacity = 64
quad = 4
steps = capacity // quad
band = 9 * channels
depth = 10 * band
face_n = 16
corner_n = 4
side_n = face_n + 2 * corner_n
base_xm = capacity
base_xp = base_xm + face_n
base_ym = base_xp + face_n
base_yp = base_ym + side_n
zero_row = base_yp + side_n
table_rows = zero_row + 1
place_base = (
    base_ym + face_n,
    base_xm,
    base_yp + face_n,
    base_ym,
    0,
    base_yp,
    base_ym + face_n + corner_n,
    base_xp,
    base_yp + face_n + corner_n,
)
vmem = pl.BlockSpec(memory_space=pltpu.VMEM)
smem = pl.BlockSpec(memory_space=pltpu.SMEM)
bf16 = jnp.bfloat16
f32 = jnp.float32


def params():
    return pltpu.CompilerParams(vmem_limit_bytes=60 * 1024 * 1024)


def octant_matrix():
    out = np.zeros((512, 512), np.float32)
    for o in range(8):
        a, b, c = o // 4, o // 2 % 2, o % 2
        for v in range(64):
            x, y, z = v // 16, v // 4 % 4, v % 4
            out[(4 * a + x) * 64 + (4 * b + y) * 8 + 4 * c + z, o * 64 + v] = 1
    return out


def upsample_matrix():
    out = np.zeros((64, 512), np.float32)
    for p in range(512):
        x, y, z = p // 64, p // 8 % 8, p % 8
        out[(x // 2) * 16 + (y // 2) * 4 + z // 2, p] = 1
    wide = np.zeros((128, 1024), np.float32)
    wide[:64, :512] = out
    wide[64:, 512:] = out
    return wide


def y_face_matrix(y):
    out = np.zeros((512, 64), np.float32)
    for x in range(8):
        for z in range(8):
            out[x * 64 + y * 8 + z, x * 8 + z] = 1
    wide = np.zeros((1024, 128), np.float32)
    wide[:512, :64] = out
    wide[512:, 64:] = out
    return wide


def pool_matrix():
    out = np.zeros((4, 2, 128, 256), np.float32)
    for t in range(4):
        for b in range(4):
            for y in range(0, 8, 2):
                for z in range(0, 8, 2):
                    out[t, b // 2, (b % 2) * 64 + y * 8 + z, b * 64 + t * 16 + (y // 2) * 4 + z // 2] = 1
    return out.reshape(1024, 256)


def const(values):
    return jnp.asarray(values, dtype=bf16)


def lane_id(rows):
    return lax.broadcasted_iota(jnp.int32, (rows, 128), 1)


def roll(v, shift):
    return pltpu.roll(v, shift % 128, 1)


def octant_kernel(send, coarse, perm, out, tab):
    low = lane_id(16) < 64
    y = jnp.dot(coarse[...].reshape(256, 512), perm[...], preferred_element_type=f32).astype(bf16)
    for i in range(8):
        for g in range(4):
            part = y[i * 32 : i * 32 + 32, g * 128 : g * 128 + 128]
            tab[i * 8 + 2 * g] = jnp.where(low, part[:16], roll(part[16:], 64))
            tab[i * 8 + 2 * g + 1] = jnp.where(low, roll(part[:16], 64), part[16:])

    def body(i, carry):
        for j in range(8):
            d = i * 8 + j
            out[d] = tab[jnp.maximum(send[d], 0)]
        return carry

    lax.fori_loop(0, 16, body, 0)


def emit_faces(lists, bricks, ylow, yhigh, out_xm, out_xp, out_ym, out_yp, wide):
    low = lane_id(16) < 64
    for r in range(side_n):
        s = lists[r]
        out_xm[r] = jnp.where(low, bricks[s, 0:16, 0:128], roll(bricks[s, 16:32, 0:128], 64))
        s = lists[side_n + r]
        out_xp[r] = jnp.where(low, roll(bricks[s, 0:16, 384:512], 64), bricks[s, 16:32, 384:512])
    for side, (matrix, out) in enumerate(((ylow, out_ym), (yhigh, out_yp))):
        for r in range(face_n):
            s = lists[2 * side_n + side * face_n + r]
            wide[r * 16 : r * 16 + 16, 0:512] = bricks[s, 0:16, :]
            wide[r * 16 : r * 16 + 16, 512:1024] = bricks[s, 16:32, :]
        out[...] = (
            jnp.dot(wide[...], matrix[...], preferred_element_type=f32)
            .astype(bf16)
            .reshape(face_n, 16, 128)
        )


def hidden_kernel(
    child, alive, lists, incoming, fine, up, ylow, yhigh, hidden, xm, xp, ym, yp, wide, full
):
    step = pl.program_id(0)
    rows = []
    for j in range(16):
        rows.append(incoming[jnp.maximum(child[step * 16 + j], 0)])
    big = jnp.dot(jnp.concatenate(rows, axis=0), up[...], preferred_element_type=f32)
    for j in range(16):
        s = step * 16 + j
        live = (alive[s] > 0).astype(f32)
        for h in range(2):
            total = fine[j, h * 16 : h * 16 + 16, :].astype(f32) + big[
                j * 16 : j * 16 + 16, h * 512 : h * 512 + 512
            ]
            value = (total * live).astype(bf16)
            hidden[j, h * 16 : h * 16 + 16, :] = value
            full[s, h * 16 : h * 16 + 16, :] = value

    @pl.when(step == pl.num_programs(0) - 1)
    def _():
        emit_faces(lists, full, ylow, yhigh, xm, xp, ym, yp, wide)


def fill_table(table, own, rxm, rxp, rym, ryp, elow, ehigh):
    def copy(i, carry):
        for j in range(8):
            table[i * 8 + j] = own[i * 8 + j]
        return carry

    lax.fori_loop(0, capacity // 8, copy, 0)
    for row, source, at in (
        [(base_xm + r, rxm, r) for r in range(face_n)]
        + [(base_ym + face_n + r, rym, face_n + r) for r in range(corner_n)]
        + [(base_yp + face_n + r, ryp, face_n + r) for r in range(corner_n)]
    ):
        table[row, 0:16, 384:512] = roll(source[at], 64)
        table[row, 16:32, 384:512] = source[at]
    for row, source, at in (
        [(base_xp + r, rxp, r) for r in range(face_n)]
        + [(base_ym + face_n + corner_n + r, rym, face_n + corner_n + r) for r in range(corner_n)]
        + [(base_yp + face_n + corner_n + r, ryp, face_n + corner_n + r) for r in range(corner_n)]
    ):
        table[row, 0:16, 0:128] = source[at]
        table[row, 16:32, 0:128] = roll(source[at], 64)
    for base, source, matrix in ((base_ym, rym, ehigh), (base_yp, ryp, elow)):
        big = jnp.dot(
            source[0:face_n].reshape(face_n * 16, 128), matrix[...], preferred_element_type=f32
        ).astype(bf16)
        for r in range(face_n):
            table[base + r, 0:16, :] = big[r * 16 : r * 16 + 16, 0:512]
            table[base + r, 16:32, :] = big[r * 16 : r * 16 + 16, 512:1024]
    table[zero_row] = jnp.zeros((channels, 512), bf16)


def to_pair(even_odd, low):
    first, second = even_odd
    return (
        jnp.where(low, first, roll(second, 64)),
        jnp.where(low, roll(first, 64), second),
    )


def shift_matrix():
    out = np.zeros((256, 256), np.float32)
    for lane in range(128):
        z = lane % 8
        out[lane - 1 if z > 0 else 128 + lane + 7, lane] = 1
        out[lane + 1 if z < 7 else 128 + lane - 7, 128 + lane] = 1
    return out


def build_stack(index, near, table, shift, kinds, turned, stack):
    lane = lane_id(channels)
    inner = lane & 63
    low = lane < 64
    y_first, y_last = inner < 8, inner >= 56
    z_last = (lane & 7) == 7

    def sources(brick, off_x, tile):
        def at(off_y, off_z):
            row = near[brick * 27 + (off_x + 1) * 9 + (off_y + 1) * 3 + off_z + 1]
            return table[row, :, tile * 128 : tile * 128 + 128]

        return (
            at(0, 0),
            jnp.where(z_last, at(0, -1), at(0, 1)),
            jnp.where(y_last, at(-1, 0), at(1, 0)),
            jnp.where(
                y_last,
                jnp.where(z_last, at(-1, -1), at(-1, 1)),
                jnp.where(z_last, at(1, -1), at(1, 1)),
            ),
        )

    for pair in range(2):
        b0 = index * quad + 2 * pair
        for off_x, tile in ((-1, 3), (0, 0), (0, 1), (0, 2), (0, 3), (1, 0)):
            first = sources(b0, off_x, tile)
            second = sources(b0 + 1, off_x, tile)
            for kind in range(4):
                swap = kind >= 2
                even, odd = to_pair(
                    (second[kind], first[kind]) if swap else (first[kind], second[kind]), low
                )
                base = (2 * pair + kind // 2) * 320
                at_lane = (kind % 2) * 128
                if off_x <= 0:
                    row = base + (0 if off_x < 0 else 2 + 2 * tile) * channels
                    kinds[row : row + channels, at_lane : at_lane + 128] = odd
                if off_x >= 0:
                    row = base + (9 if off_x > 0 else 1 + 2 * tile) * channels
                    kinds[row : row + channels, at_lane : at_lane + 128] = even
    turned[...] = jnp.dot(kinds[...], shift[...], preferred_element_type=f32).astype(bf16)
    for pair in range(2):
        for plane in range(10):
            own_row = 2 * pair * 320 + plane * channels
            far_row = own_row + 320
            for k in range(3):
                source, at_lane = ((turned, 0), (kinds, 0), (turned, 128))[k]
                own = source[own_row : own_row + channels, at_lane : at_lane + 128]
                far = source[far_row : far_row + channels, at_lane : at_lane + 128]
                trio = (
                    roll(jnp.where(y_last, far, own), 8),
                    own,
                    roll(jnp.where(y_first, far, own), -8),
                )
                for j in range(3):
                    row = plane * band + (j * 3 + k) * channels
                    stack[row : row + channels, pair * 128 : pair * 128 + 128] = trio[j]


def banded(taps, weight):
    weight[...] = jnp.zeros_like(weight)
    for x in range(8):
        weight[x * 32 : x * 32 + 32, x * band : x * band + 3 * band] = taps[...]


def convolve(weight, stack):
    halves = []
    for h in range(2):
        seen = slice(h * 4 * band, h * 4 * band + 6 * band)
        halves.append(
            jnp.dot(weight[h * 128 : h * 128 + 128, seen], stack[seen], preferred_element_type=f32)
        )
    return jnp.concatenate(halves, axis=0)


def alive_lanes(step, near):
    lane = lax.broadcasted_iota(jnp.int32, (1, 256), 1)
    out = jnp.zeros((1, 256), f32)
    for i in range(quad):
        live = (near[(step * quad + i) * 27 + 13] != zero_row).astype(f32)
        out = jnp.where(lane // 64 == i, live, out)
    return out


def quad_cotangent(cot, at, t, low):
    even, odd = [], []
    for pair in range(2):
        e, o = to_pair(
            (
                cot[at + 2 * pair, :, t * 128 : t * 128 + 128],
                cot[at + 2 * pair + 1, :, t * 128 : t * 128 + 128],
            ),
            low,
        )
        even.append(e)
        odd.append(o)
    return (
        jnp.concatenate(even, axis=1).astype(f32),
        jnp.concatenate(odd, axis=1).astype(f32),
    )


def from_pair(ref, at, even, odd, t, low):
    for pair in range(2):
        e = even[:, pair * 128 : pair * 128 + 128]
        o = odd[:, pair * 128 : pair * 128 + 128]
        ref[at + 2 * pair, :, t * 128 : t * 128 + 128] = jnp.where(low, e, roll(o, 64))
        ref[at + 2 * pair + 1, :, t * 128 : t * 128 + 128] = jnp.where(low, roll(e, 64), o)


def forward_kernel(
    near, lists, hidden, rxm, rxp, rym, ryp, cot, taps, elow, ehigh, ylow, yhigh, shift,
    block_out, grad, term, xm, xp, ym, yp,
    table, weight, wide, kinds, turned, stacks, total, term_wide,
):
    step = pl.program_id(0)

    def build(index, slot):
        build_stack(index, near, table, shift, kinds[slot], turned[slot], stacks[slot])

    @pl.when(step == 0)
    def _():
        banded(taps, weight)
        fill_table(table, hidden, rxm, rxp, rym, ryp, elow, ehigh)
        total[...] = jnp.zeros_like(total)
        build(0, 0)

    low = lane_id(channels) < 64

    def process(index, slot):
        stack = stacks[slot]
        pre_all = convolve(weight, stack)
        live = alive_lanes(index, near)
        grad_pair = []
        for t in range(4):
            cots = quad_cotangent(cot, slot * quad, t, low)
            mixed, grads = [], []
            for p in range(2):
                x = 2 * t + p
                pre = pre_all[x * 32 : x * 32 + 32]
                row = (x + 1) * band + 4 * channels
                here = stack[row : row + channels, :].astype(f32)
                sigma = 0.5 * jnp.tanh(0.5 * pre) + 0.5
                mixed.append(((here + pre * sigma) * live).astype(bf16))
                grads.append((cots[p] * (sigma * (1.0 + pre * (1.0 - sigma))) * live).astype(bf16))
            from_pair(block_out, slot * quad, mixed[0], mixed[1], t, low)
            from_pair(grad, index * quad, grads[0], grads[1], t, low)
            grad_pair += grads
        grad_all = jnp.concatenate(grad_pair, axis=0)
        for x in range(10):
            total[x * band : x * band + band] += lax.dot_general(
                stack[x * band : x * band + band],
                grad_all,
                (((1,), (1,)), ((), ())),
                preferred_element_type=f32,
            )

    build(2 * step + 1, 1)
    process(2 * step, 0)
    build(jnp.minimum(2 * step + 2, steps - 1), 0)
    process(2 * step + 1, 1)

    @pl.when(step == steps // 2 - 1)
    def _():
        emit_faces(lists, grad, ylow, yhigh, xm, xp, ym, yp, wide)
        acc = total[0 : 3 * band, 0:32]
        for x in range(1, 8):
            acc = acc + total[x * band : x * band + 3 * band, x * 32 : x * 32 + 32]
        term_wide[...] = jnp.zeros((1024, 128), f32)
        term_wide[0 : 3 * band, 0:32] = acc
        across = term_wide[...].T
        for j in range(4):
            for half in range(2):
                at_lane = j * 256 + half * 128
                term[j * 32 : j * 32 + 32, half, :] = across[0:32, at_lane : at_lane + 128]


def backward_kernel(
    near, child, grad, rxm, rxp, rym, ryp, cot, taps, elow, ehigh, pool, shift, terms,
    fine_grad, back,
    table, weight, kinds, turned, stacks, octants,
):
    step = pl.program_id(0)

    def build(index, slot):
        build_stack(index, near, table, shift, kinds[slot], turned[slot], stacks[slot])

    @pl.when(step == 0)
    def _():
        banded(taps, weight)
        fill_table(table, grad, rxm, rxp, rym, ryp, elow, ehigh)
        build(0, 0)
        rest = jnp.sum(terms[...], axis=0)
        rows = []
        for i in range(3):
            part = rest.astype(bf16)
            rest = rest - part.astype(f32)
            rows += [part.astype(f32)]
        rows += [jnp.zeros((2, 128), f32)]
        tail = jnp.concatenate(rows, axis=0).astype(bf16)
        clear = jnp.zeros((16, 128), bf16)

        def body(i, carry):
            for j in range(8):
                back[i * 8 + j, 0:16, :] = clear
                back[i * 8 + j, 16:24, :] = tail
            return carry

        lax.fori_loop(0, 16, body, 0)

    low = lane_id(channels) < 64
    low16 = lane_id(16) < 64

    def process(index, slot):
        conv = convolve(weight, stacks[slot])
        live = alive_lanes(index, near)
        sums = []
        for t in range(4):
            cots = quad_cotangent(cot, slot * quad, t, low)
            full = [
                (cots[p] + conv[(2 * t + p) * 32 : (2 * t + p) * 32 + 32]) * live
                for p in range(2)
            ]
            from_pair(fine_grad, slot * quad, full[0].astype(bf16), full[1].astype(bf16), t, low)
            both = full[0] + full[1]
            for pair in range(2):
                v = both[:, pair * 128 : pair * 128 + 128]
                v = v + roll(v, -1)
                v = v + roll(v, -8)
                sums.append(v.astype(bf16))
        rows = pl.ds(pl.multiple_of(index * channels, channels), channels)
        for i in range(8):
            octants[rows, i * 128 : i * 128 + 128] = sums[i]

    build(2 * step + 1, 1)
    process(2 * step, 0)
    process(2 * step + 1, 1)
    build(jnp.minimum(2 * step + 2, steps - 1), 0)

    @pl.when(step == steps // 2 - 1)
    def _():
        pooled = jnp.dot(octants[...], pool[...], preferred_element_type=f32).astype(bf16)
        for s in range(capacity):
            row = s // quad * channels
            at_lane = (s % quad) // 2 * 128
            tile = pooled[row : row + channels, at_lane : at_lane + 128]
            if s % 2 == 0:
                packed = jnp.where(low16, tile[:16], roll(tile[16:], 64))
            else:
                packed = jnp.where(low16, roll(tile[:16], 64), tile[16:])
            back[child[s], 0:16, :] = packed


def last_kernel(send, returned, perm, coarse_grad, weight_grad, tab, parts):
    low = lane_id(16) < 64
    tab[...] = jnp.zeros_like(tab)

    def body(i, carry):
        for j in range(8):
            d = i * 8 + j
            target = send[d]

            @pl.when(target >= 0)
            def _():
                tab[target] = returned[d, 0:16, :]

        return carry

    lax.fori_loop(0, 16, body, 0)
    rows = []
    for i in range(8):
        tops, bottoms = [], []
        for g in range(4):
            a, b = tab[i * 8 + 2 * g], tab[i * 8 + 2 * g + 1]
            tops.append(jnp.where(low, a, roll(b, 64)))
            bottoms.append(jnp.where(low, roll(a, 64), b))
        rows.append(jnp.concatenate(tops, axis=1))
        rows.append(jnp.concatenate(bottoms, axis=1))
    spread = jnp.dot(jnp.concatenate(rows, axis=0), perm[...], preferred_element_type=f32)
    coarse_grad[...] = spread.astype(bf16).reshape(8, 32, 512)
    parts[...] = returned[:, 16:24, :].astype(f32)
    for half in range(2):
        total = parts[:, half, :] + parts[:, half + 2, :] + parts[:, half + 4, :]
        for j in range(4):
            for i in range(4):
                k = j * 8 + half * 4 + i
                if k < 27:
                    weight_grad[k] = total[j * 32 : j * 32 + 32, i * 32 : i * 32 + 32]


def shape(dims, kind=bf16):
    return jax.ShapeDtypeStruct(dims, kind)


def ranks(flags):
    before = (jnp.arange(capacity)[:, None] < jnp.arange(capacity)[None, :]).astype(bf16)
    return jnp.dot(flags.astype(bf16), before, preferred_element_type=f32).astype(jnp.int32)


def indices(adjacency):
    table_id = jnp.arange(9 * capacity, dtype=jnp.int32)
    hits = adjacency[:, :, None] == table_id
    rank = ranks(hits.any(axis=(0, 1)).reshape(9, capacity)).reshape(-1)
    row_base = jnp.asarray(np.repeat(np.array(place_base), capacity), jnp.int32)
    own = (table_id // capacity) == 4
    row_of = jnp.where(own, table_id % capacity, row_base + rank)
    near = jnp.sum(jnp.where(hits, row_of, 0), axis=2)
    near = jnp.where(adjacency < 0, zero_row, near)
    place = jnp.where(adjacency < 0, -1, adjacency // capacity)
    need = (place[None, :, :] == jnp.arange(9)[:, None, None]).any(axis=2)
    order = ranks(need)
    slot = jnp.arange(capacity, dtype=jnp.int32)
    pick = need[:, None, :] & (order[:, None, :] == jnp.arange(face_n)[None, :, None])
    chosen = jnp.sum(jnp.where(pick, slot, 0), axis=2)
    lists = jnp.concatenate(
        [
            chosen[1], chosen[0, :corner_n], chosen[2, :corner_n],
            chosen[7], chosen[6, :corner_n], chosen[8, :corner_n],
            chosen[3], chosen[5],
        ]
    )
    return near.reshape(-1).astype(jnp.int32), lists.astype(jnp.int32)


def moved(value, shift_x, shift_y):
    count_x, count_y = lax.axis_size("gx"), lax.axis_size("gy")
    pairs = [
        (i * count_y + j, (i + shift_x) * count_y + j + shift_y)
        for i in range(count_x)
        for j in range(count_y)
        if 0 <= i + shift_x < count_x and 0 <= j + shift_y < count_y
    ]
    return lax.ppermute(value, axes, pairs)


def join(ym, yp, from_xm, from_xp, down, up):
    for out, plane, at in ((down, ym, face_n), (up, yp, face_n + corner_n)):
        out[0:face_n] = plane[...]
        out[face_n : face_n + corner_n] = from_xm[at : at + corner_n]
        out[face_n + corner_n : side_n] = from_xp[at : at + corner_n]


def hold_kernel(term, after, passed):
    passed[...] = term[...]


def halo(xm, xp, ym, yp, term=None):
    from_xm = moved(xp, 1, 0)
    from_xp = moved(xm, -1, 0)
    side = shape((side_n, 16, 128))
    down, up = pl.pallas_call(
        join,
        out_shape=(side, side),
        in_specs=[vmem] * 4,
        out_specs=(vmem, vmem),
        compiler_params=params(),
        name="join",
    )(ym, yp, from_xm, from_xp)
    from_ym = moved(up, 0, 1)
    from_yp = moved(down, 0, -1)
    passed = []
    if term is not None:
        passed = [
            pl.pallas_call(
                hold_kernel,
                out_shape=shape(term.shape, f32),
                in_specs=[vmem, pl.BlockSpec(memory_space=pl.ANY)],
                out_specs=vmem,
                compiler_params=params(),
                name="hold",
            )(term, down)
        ]
    return [from_xm, from_xp, from_ym, from_yp] + passed


def exchange(value):
    return lax.all_to_all(value, axes, split_axis=0, concat_axis=0, tiled=True)


def whole(dims):
    return pl.BlockSpec(dims, lambda i: (0,) * len(dims))


def on_device(fine, coarse, weight, cotangent, adjacency, send_list, child_src):
    devices = lax.axis_size("gx") * lax.axis_size("gy")
    send = send_list.reshape(-1)
    perm = const(octant_matrix())
    perm_t = const(octant_matrix().T)
    y_low, y_high = y_face_matrix(0), y_face_matrix(7)
    ylow, yhigh = const(y_low), const(y_high)
    elow, ehigh = const(y_low.T), const(y_high.T)
    up = const(upsample_matrix())
    pool = const(pool_matrix())
    shift = const(shift_matrix())
    packed = (16, 128)
    side = shape((side_n,) + packed)
    face = shape((face_n,) + packed)

    outgoing = pl.pallas_call(
        octant_kernel,
        out_shape=shape((devices,) + packed),
        in_specs=[smem, vmem, vmem],
        out_specs=vmem,
        scratch_shapes=[pltpu.VMEM((64,) + packed, bf16)],
        compiler_params=params(),
        name="octants",
    )(send, coarse, perm)
    incoming = exchange(outgoing)

    near, lists = indices(adjacency)
    alive = (adjacency[:, 13] >= 0).astype(jnp.int32)
    sender = jnp.arange(devices, dtype=jnp.int32)
    unused = jnp.where((child_src[:, None] == sender).any(axis=0), devices, sender).min()
    back_to = jnp.where(child_src < 0, unused, child_src)
    taps = weight.transpose(1, 0, 2).reshape(channels, 27 * channels)
    back_taps = weight[::-1].transpose(2, 0, 1).reshape(channels, 27 * channels)

    part = pl.BlockSpec((16, channels, 512), lambda i: (i, 0, 0))
    hidden, xm, xp, ym, yp = pl.pallas_call(
        hidden_kernel,
        grid=(capacity // 16,),
        out_shape=(shape((capacity, channels, 512)), side, side, face, face),
        in_specs=[smem, smem, smem, whole((devices,) + packed), part]
        + [whole((128, 1024))]
        + [whole((1024, 128))] * 2,
        out_specs=(part,) + tuple(whole((n,) + packed) for n in (side_n, side_n, face_n, face_n)),
        scratch_shapes=[
            pltpu.VMEM((face_n * 16, 1024), bf16),
            pltpu.VMEM((capacity, channels, 512), bf16),
        ],
        compiler_params=params(),
        name="hidden",
    )(child_src, alive, lists, incoming, fine, up, ylow, yhigh)
    near_h = halo(xm, xp, ym, yp)

    bricks = whole((capacity, channels, 512))
    sides = [whole((side_n,) + packed)] * 4
    per_step = pl.BlockSpec((2 * quad, channels, 512), lambda i: (i, 0, 0))
    table = pltpu.VMEM((table_rows, channels, 512), bf16)
    wide = pltpu.VMEM((face_n * 16, 1024), bf16)
    banded_weight = pltpu.VMEM((256, depth), bf16)
    work = [
        [pltpu.VMEM((1280, 256), bf16)] * 2,
        [pltpu.VMEM((1280, 256), bf16)] * 2,
        [pltpu.VMEM((depth, 256), bf16)] * 2,
    ]
    block_out, grad, term, gxm, gxp, gym, gyp = pl.pallas_call(
        forward_kernel,
        grid=(steps // 2,),
        out_shape=(
            shape((capacity, channels, 512)),
            shape((capacity, channels, 512)),
            shape((devices, 2, 128), f32),
            side, side, face, face,
        ),
        in_specs=[smem, smem, bricks]
        + sides
        + [per_step, whole((channels, 27 * channels))]
        + [whole((128, 1024))] * 2
        + [whole((1024, 128))] * 2
        + [whole((256, 256))],
        out_specs=(per_step, bricks, whole((devices, 2, 128)))
        + tuple(whole((n,) + packed) for n in (side_n, side_n, face_n, face_n)),
        scratch_shapes=[table, banded_weight, wide]
        + work
        + [pltpu.VMEM((depth, 256), f32), pltpu.VMEM((1024, 128), f32)],
        compiler_params=params(),
        name="forward",
    )(near, lists, hidden, *near_h, cotangent, taps, elow, ehigh, ylow, yhigh, shift)
    *near_g, term = halo(gxm, gxp, gym, gyp, term)
    terms = exchange(term)

    fine_grad, back = pl.pallas_call(
        backward_kernel,
        grid=(steps // 2,),
        out_shape=(shape((capacity, channels, 512)), shape((devices, 24, 128))),
        in_specs=[smem, smem, bricks]
        + sides
        + [per_step, whole((channels, 27 * channels)), whole((128, 1024)), whole((128, 1024))]
        + [whole((1024, 256)), whole((256, 256)), whole((devices, 2, 128))],
        out_specs=(per_step, whole((devices, 24, 128))),
        scratch_shapes=[table, banded_weight] + work + [pltpu.VMEM((steps * channels, 1024), bf16)],
        compiler_params=params(),
        name="backward",
    )(near, back_to, grad, *near_g, cotangent, back_taps, elow, ehigh, pool, shift, terms)
    returned = exchange(back)

    coarse_grad, weight_grad = pl.pallas_call(
        last_kernel,
        out_shape=(shape((8, channels, 512)), shape((27, channels, channels), f32)),
        in_specs=[smem, vmem, vmem],
        out_specs=(vmem, vmem),
        scratch_shapes=[pltpu.VMEM((64,) + packed, bf16), pltpu.VMEM((devices, 8, 128), f32)],
        compiler_params=params(),
        name="coarse",
    )(send, returned, perm_t)
    return block_out, fine_grad, coarse_grad, weight_grad


def solution(mesh):
    return jax.shard_map(
        on_device,
        mesh=mesh,
        in_specs=(
            P(axes, None, None),
            P(axes, None, None),
            P(),
            P(axes, None, None),
            P(axes, None),
            P(axes, None),
            P(axes),
        ),
        out_specs=(
            P(axes, None, None),
            P(axes, None, None),
            P(axes, None, None),
            P(),
        ),
        check_vma=False,
    )
```
